512 devices in a mesh: tm: 32 (over z_lo, x, core), space: 16 (over y, z_hi).
Axes of the slice: x: 4, y: 4, z: 16 (z_hi: 4, z_lo: 4; z = z_hi * 4 + z_lo), core: 2. Of those that a mesh axis runs over, the one named last changes fastest.
Arguments:
- queries: bfloat16 [32, 256, 8, 512], P('tm', 'space'), may hold values from -6 to 6
- key_vectors: bfloat16 [32, 256, 8, 512], P('tm', 'space'), may hold values from -6 to 6
- values: bfloat16 [32, 256, 8, 512], P('tm', 'space'), may hold values from -6 to 6
- cotangent: bfloat16 [32, 256, 8, 512], P('tm', 'space'), may hold values from -6 to 6
- dilation: int32 [8], replicated, may hold values from 1 to 4, as said below
Outputs:
- attended: bfloat16 [32, 256, 8, 512], P('tm', 'space')
- grad_queries: bfloat16 [32, 256, 8, 512], P('tm', 'space')
- grad_keys: bfloat16 [32, 256, 8, 512], P('tm', 'space')
- grad_values: bfloat16 [32, 256, 8, 512], P('tm', 'space')
The draws below stay inside these ranges and needn't reach their ends.
Inputs may be any that keep to these rules, and one draw needn't show every extreme that they name: Exactly 2 heads have dilation 1, 2 have dilation 2 and the others 4; which heads is drawn.
All inputs are finite; a program needn't handle non-finite values.
Results may differ from the reference program's by a relative error of at most 0.034.
Values may be sent and summed in bfloat16 or wider, within the bound.
A program may use at most 128 MiB of HBM per device.

```python
import jax
import jax.numpy as jnp
from jax import lax

HEADS = 8
HEAD_DIM = 64
KERNEL = 7
FRAMES_DEV = 1
ROWS_DEV = 16
COLS = 8
D = 512
NF = 32
NR = 256


def draw_queries(key, part):
    own_key = jax.random.fold_in(key, 3)
    return jnp.clip(jax.random.normal(own_key, (NF, NR, COLS, D)), -6.0, 6.0).astype(jnp.bfloat16)


def draw_key_vectors(key, part):
    own_key = jax.random.fold_in(key, 5)
    return jnp.clip(jax.random.normal(own_key, (NF, NR, COLS, D)), -6.0, 6.0).astype(jnp.bfloat16)


def draw_dilation(key, part):
    own_key = jax.random.fold_in(key, 7)
    quarter = HEADS // 4
    ladder = jnp.concatenate([jnp.ones((quarter,), jnp.int32), 2 * jnp.ones((quarter,), jnp.int32), 4 * jnp.ones((HEADS - 2 * quarter,), jnp.int32)])
    shuffle = jax.random.permutation(own_key, HEADS)
    return jnp.take(ladder, shuffle).astype(jnp.int32)


def levels(stream_key, dims, cuts, low, high):
    factor_of, own = 1.0, jax.random.fold_in(stream_key, 6)
    for position, parts in cuts:
        heights = jnp.exp(jax.random.uniform(jax.random.fold_in(own, position), (parts,), jnp.float32, low / len(cuts), high / len(cuts)))
        factor_of = factor_of * jnp.repeat(heights, dims[position] // parts).reshape([-1 if axis == position else 1 for axis in range(len(dims))])
    return factor_of


def normal_values(stream_key, shape, width, bound, split=(), kind=jnp.bfloat16):
    values = jax.random.normal(stream_key, shape, jnp.float32) * width
    if len(split) > 0:
        values = levels(stream_key, shape, split, -0.22, 0.18) * values
    return jnp.clip(values, min=-bound, max=bound).astype(kind)


def setup_inputs(seed: int = 0) -> dict:
    seeds = jax.random.split(jax.random.key(seed), 6)
    queries = draw_queries(jax.random.fold_in(seeds[5], 71), 0)
    key_vectors = draw_key_vectors(jax.random.fold_in(seeds[5], 71), 0)
    values = normal_values(seeds[2], (NF, NR, COLS, D), 1.0, 6.0, ((0, 32), (1, 16)))
    cotangent = normal_values(seeds[3], (NF, NR, COLS, D), 1.0, 6.0, ((0, 32), (1, 16)))
    dilation = draw_dilation(jax.random.fold_in(seeds[5], 71), 0)
    return {"queries": queries, "key_vectors": key_vectors, "values": values, "cotangent": cotangent, "dilation": dilation}


def neighbour_mask(frame_count, row_count, col_count, frame_reach, row_reach, dilation_step, frame_start, row_start, total_frames, total_rows):
    query_frame = jnp.broadcast_to(jnp.arange(frame_count, dtype=jnp.int32).reshape(-1, 1, 1), (frame_count, row_count, col_count)).reshape(-1)
    query_row = jnp.broadcast_to(jnp.arange(row_count, dtype=jnp.int32).reshape(1, -1, 1), (frame_count, row_count, col_count)).reshape(-1)
    query_col = jnp.broadcast_to(jnp.arange(col_count, dtype=jnp.int32).reshape(1, 1, -1), (frame_count, row_count, col_count)).reshape(-1)
    key_frames = frame_count + 2 * frame_reach
    key_rows = row_count + 2 * row_reach
    key_frame = jnp.broadcast_to(jnp.arange(key_frames, dtype=jnp.int32).reshape(-1, 1, 1), (key_frames, key_rows, col_count)).reshape(-1)
    key_row = jnp.broadcast_to(jnp.arange(key_rows, dtype=jnp.int32).reshape(1, -1, 1), (key_frames, key_rows, col_count)).reshape(-1)
    key_col = jnp.broadcast_to(jnp.arange(col_count, dtype=jnp.int32).reshape(1, 1, -1), (key_frames, key_rows, col_count)).reshape(-1)
    delta_frame = key_frame[None, :] - frame_reach - query_frame[:, None]
    delta_row = key_row[None, :] - row_reach - query_row[:, None]
    delta_col = key_col[None, :] - query_col[:, None]
    allowed = (jnp.abs(delta_frame) <= frame_reach) & (jnp.abs(delta_row) <= row_reach) & (jnp.abs(delta_col) <= row_reach)
    allowed = allowed & (jnp.remainder(delta_row, dilation_step) == 0) & (jnp.remainder(delta_col, dilation_step) == 0)
    global_frame = frame_start + key_frame - frame_reach
    global_row = row_start + key_row - row_reach
    inside = (global_frame >= 0) & (global_frame < total_frames) & (global_row >= 0) & (global_row < total_rows)
    return allowed & inside[None, :]


def masked_scores(query_block, key_block, allowed):
    scores = jnp.einsum("qhe,khe->hqk", query_block.astype(jnp.float32), key_block.astype(jnp.float32)) * (HEAD_DIM ** -0.5)
    return jnp.where(allowed[None], scores, -1e30)


def as_index(values_list):
    return tuple(jnp.asarray(entry, dtype=jnp.int32) for entry in values_list)


def reference(queries, key_vectors, values, cotangent, dilation):
    head_count = dilation.shape[0]
    head_size = D // head_count
    head_order = jnp.argsort(dilation, stable=True).astype(jnp.int32)
    head_restore = jnp.argsort(head_order, stable=True).astype(jnp.int32)

    def sort_heads(array, permutation):
        return jnp.take(array.reshape(NF, NR, COLS, head_count, head_size), permutation, axis=3)

    sorted_query = sort_heads(queries, head_order)
    sorted_grad = sort_heads(cotangent, head_order)
    frame_reach = KERNEL // 2
    pad_rows = frame_reach * 4
    padding = ((frame_reach, frame_reach), (pad_rows, pad_rows), (0, 0), (0, 0), (0, 0))
    padded_keys = jnp.pad(sort_heads(key_vectors, head_order), padding)
    padded_values = jnp.pad(sort_heads(values, head_order), padding)
    quarter = head_count // 4
    groups = ((1, 0, quarter), (2, quarter, quarter), (4, 2 * quarter, head_count - 2 * quarter))
    row_blocks = NR // ROWS_DEV
    block_total = (NF // FRAMES_DEV) * row_blocks

    def one_block(running, block_index):
        key_grad, value_grad = running
        frame_start = (block_index // row_blocks) * FRAMES_DEV
        row_start = (block_index % row_blocks) * ROWS_DEV
        extent = (FRAMES_DEV, ROWS_DEV, COLS, head_count, head_size)
        query_all = lax.dynamic_slice(sorted_query, as_index((frame_start, row_start, 0, 0, 0)), extent)
        grad_all = lax.dynamic_slice(sorted_grad, as_index((frame_start, row_start, 0, 0, 0)), extent)
        attended_parts = []
        grad_query_parts = []
        for dilation_step, first_head, group_size in groups:
            row_reach = frame_reach * dilation_step
            anchor = as_index((frame_start, row_start + pad_rows - row_reach, 0, first_head, 0))
            tile_extent = (FRAMES_DEV + 2 * frame_reach, ROWS_DEV + 2 * row_reach, COLS, group_size, head_size)
            key_block = lax.dynamic_slice(padded_keys, anchor, tile_extent).reshape(-1, group_size, head_size)
            value_block = lax.dynamic_slice(padded_values, anchor, tile_extent).reshape(-1, group_size, head_size)
            query_block = query_all[:, :, :, first_head:first_head + group_size, :].reshape(-1, group_size, head_size)
            grad_block = grad_all[:, :, :, first_head:first_head + group_size, :].reshape(-1, group_size, head_size)
            allowed = neighbour_mask(FRAMES_DEV, ROWS_DEV, COLS, frame_reach, row_reach, dilation_step, frame_start, row_start, NF, NR)
            scores = masked_scores(query_block, key_block, allowed)
            row_peak = jnp.max(scores, axis=-1, keepdims=True)
            row_total = jnp.sum(jnp.exp(scores - row_peak), axis=-1, keepdims=True)
            weights = jnp.exp(scores - row_peak) / row_total
            weights_low = weights.astype(jnp.bfloat16)
            attended_block = jnp.einsum("hqk,khe->qhe", weights_low.astype(jnp.float32), value_block.astype(jnp.float32)).astype(jnp.bfloat16)
            delta = jnp.sum(grad_block.astype(jnp.float32) * attended_block.astype(jnp.float32), axis=-1)
            grad_weights = jnp.einsum("qhe,khe->hqk", grad_block.astype(jnp.float32), value_block.astype(jnp.float32))
            grad_scores = (weights * (grad_weights - jnp.transpose(delta)[:, :, None])).astype(jnp.bfloat16)
            grad_query_block = jnp.einsum("hqk,khe->qhe", grad_scores.astype(jnp.float32), key_block.astype(jnp.float32)) * (HEAD_DIM ** -0.5)
            grad_key_block = jnp.einsum("hqk,qhe->khe", grad_scores.astype(jnp.float32), query_block.astype(jnp.float32)) * (HEAD_DIM ** -0.5)
            grad_value_block = jnp.einsum("hqk,qhe->khe", weights_low.astype(jnp.float32), grad_block.astype(jnp.float32))
            key_grad = lax.dynamic_update_slice(key_grad, lax.dynamic_slice(key_grad, anchor, tile_extent) + grad_key_block.reshape(tile_extent), anchor)
            value_grad = lax.dynamic_update_slice(value_grad, lax.dynamic_slice(value_grad, anchor, tile_extent) + grad_value_block.reshape(tile_extent), anchor)
            attended_parts.append(attended_block)
            grad_query_parts.append(grad_query_block)
        attended_here = jnp.concatenate(attended_parts, axis=1).reshape(extent)
        grad_query_here = jnp.concatenate(grad_query_parts, axis=1).reshape(extent)
        return (key_grad, value_grad), (attended_here, grad_query_here)

    padded_shape = (NF + 2 * frame_reach, NR + 2 * pad_rows, COLS, head_count, head_size)
    start_state = (jnp.zeros(padded_shape, jnp.float32), jnp.zeros(padded_shape, jnp.float32))
    final_state, stacked_out = lax.scan(one_block, start_state, jnp.arange(block_total, dtype=jnp.int32))

    def unblock(array):
        shaped = array.reshape(NF // FRAMES_DEV, row_blocks, FRAMES_DEV, ROWS_DEV, COLS, head_count, head_size)
        shaped = jnp.transpose(shaped, (0, 2, 1, 3, 4, 5, 6)).reshape(NF, NR, COLS, head_count, head_size)
        return jnp.take(shaped, head_restore, axis=3).reshape(NF, NR, COLS, D)

    def unpad(array):
        inner = array[frame_reach:frame_reach + NF, pad_rows:pad_rows + NR]
        return jnp.take(inner, head_restore, axis=3).reshape(NF, NR, COLS, D).astype(jnp.bfloat16)

    attended = unblock(stacked_out[0])
    grad_queries = unblock(stacked_out[1]).astype(jnp.bfloat16)
    return attended, grad_queries, unpad(final_state[0]), unpad(final_state[1])
```

```python
import functools

import jax
import jax.numpy as jnp
from jax import lax
from jax.experimental import pallas as pl
from jax.experimental.pallas import tpu as pltpu
from jax.sharding import PartitionSpec as P

HEADS = 8
WIDTH = 64
ROWS = 16
COLS = 8
RING = 8
REACH = 3
SPAN = 16
CELL = ROWS * COLS
HALO = 12
EDGE = HALO * COLS
MESH = pl.DeviceIdType.MESH
F32 = jnp.float32
BF16 = jnp.bfloat16

HALO_ROWS = (12, 12, 12, 12, 4, 4, 6, 6)
GROUP_ROWS = (12, 4, 6)


def slot_device(slot):
    return 2 * lax.rem(slot, 4) + lax.div(slot, 4)


def head_ranks(dilation):
    steps = [dilation[h] for h in range(HEADS)]
    ranks = []
    for h in range(HEADS):
        rank = jnp.int32(0)
        for other in range(HEADS):
            before = steps[other] <= steps[h] if other < h else steps[other] < steps[h]
            if other != h:
                rank = rank + jnp.where(before, 1, 0)
        ranks.append(rank)
    return ranks


def low_lanes(rows):
    return lax.broadcasted_iota(jnp.int32, (rows, 2 * WIDTH), 1) < WIDTH


def pack_kernel(dilation, query, key, value, grad, packed):
    ranks = head_ranks(dilation)
    low = low_lanes(CELL)
    for slot in range(HEADS):
        head = jnp.int32(0)
        for h in range(HEADS):
            head = head + jnp.where(ranks[h] == (slot + 4) % HEADS, h, 0)
        odd = lax.rem(head, 2) == 1
        lanes = pl.ds(pl.multiple_of(lax.div(head, 2) * 2 * WIDTH, 2 * WIDTH), 2 * WIDTH)
        for place, (first, second) in enumerate(((key, value), (query, grad))):
            a = first[:, lanes].astype(F32)
            b = second[:, lanes].astype(F32)
            a = jnp.where(odd, pltpu.roll(a, WIDTH, 1), a)
            b = jnp.where(odd, b, pltpu.roll(b, WIDTH, 1))
            packed[slot, place] = jnp.where(low, a, b).astype(BF16)


def unpack_kernel(dilation, result, attended, grad_query, grad_key, grad_value):
    ranks = head_ranks(dilation)
    low = low_lanes(CELL)
    for block in range(HEADS // 2):
        slots = [lax.rem(ranks[2 * block + i] + 4, HEADS) for i in range(2)]
        lanes = pl.ds(block * 2 * WIDTH, 2 * WIDTH)
        for place, (first, second) in enumerate(((grad_key, grad_value), (grad_query, attended))):
            a = result[slots[0], place].astype(F32)
            b = result[slots[1], place].astype(F32)
            first[:, lanes] = jnp.where(low, a, pltpu.roll(b, WIDTH, 1)).astype(BF16)
            second[:, lanes] = jnp.where(low, pltpu.roll(a, WIDTH, 1), b).astype(BF16)


def for_each(count, body):
    def step(i, carry):
        body(i)
        return carry

    lax.fori_loop(0, count, step, 0)


def main_kernel(
    rings,
    blocks,
    packed,
    result,
    halo,
    main,
    hstage,
    keys,
    quers,
    bias,
    scores,
    probs,
    total,
    gmain,
    ghalo,
    rmain,
    rmain_b,
    rhalo,
    rhalo_b,
    hsum,
    rrow,
    final,
    row_send,
    row_recv,
    main_send,
    main_next,
    main_recv,
    halo_send,
    halo_next,
    halo_recv,
    gmain_send,
    gmain_recv,
    gmain_recv_b,
    ghalo_send,
    ghalo_recv,
    ghalo_recv_b,
    back_send,
    back_recv,
):
    tm = lax.axis_index("tm")
    space = lax.axis_index("space")
    ring = lax.div(tm, RING)
    me = lax.rem(tm, RING)
    my_slot = lax.rem(me, 2) * 4 + lax.div(me, 2)
    group = jnp.where(lax.rem(me, 2) == 0, 0, jnp.where(me < 4, 1, 2))
    step = jnp.where(group == 0, 4, group)
    has_down = ring > 0
    has_up = ring < rings - 1
    has_prev = space > 0
    has_next = space < blocks - 1
    to_down = has_down & (me <= 2)
    to_up = has_up & (me >= 5)
    shared = to_down | to_up

    def by_group(body):
        for number, rows in enumerate(GROUP_ROWS):
            pl.when(group == number)(functools.partial(body, rows))

    def send(source, target, send_sem, recv_sem, where):
        return pltpu.make_async_remote_copy(
            src_ref=source,
            dst_ref=target,
            send_sem=send_sem,
            recv_sem=recv_sem,
            device_id=where,
            device_id_type=MESH,
        )

    def arrived(ref, sem):
        pltpu.make_async_copy(ref, ref, sem).wait()

    barrier = pltpu.get_barrier_semaphore()

    def greet(i):
        def hello(where):
            pl.semaphore_signal(barrier, inc=1, device_id=where, device_id_type=MESH)

        pl.when(i != me)(lambda: hello({"tm": ring * RING + i}))
        pl.when(has_down & ((me <= 2) | (i >= 5)))(lambda: hello({"tm": (ring - 1) * RING + i}))
        pl.when(has_up & ((me >= 5) | (i <= 2)))(lambda: hello({"tm": (ring + 1) * RING + i}))

    for_each(RING, greet)

    @pl.when(has_prev)
    def _():
        pl.semaphore_signal(barrier, inc=1, device_id={"space": space - 1}, device_id_type=MESH)

    @pl.when(has_next)
    def _():
        pl.semaphore_signal(barrier, inc=1, device_id={"space": space + 1}, device_id_type=MESH)

    greeted = (
        RING
        - 1
        + jnp.where(has_down, jnp.where(me <= 2, RING, 3), 0)
        + jnp.where(has_up, jnp.where(me >= 5, RING, 3), 0)
        + jnp.where(has_prev, 1, 0)
        + jnp.where(has_next, 1, 0)
    )
    pl.semaphore_wait(barrier, greeted)

    def row_copies(slot):
        size = HALO_ROWS[slot] * COLS
        upward = send(
            packed.at[slot, 0, pl.ds(CELL - size, size)],
            halo.at[slot, pl.ds(EDGE - size, size)],
            row_send.at[slot, 0],
            row_recv.at[slot, 0],
            {"space": space + 1},
        )
        downward = send(
            packed.at[slot, 0, pl.ds(0, size)],
            halo.at[slot, pl.ds(EDGE, size)],
            row_send.at[slot, 1],
            row_recv.at[slot, 1],
            {"space": space - 1},
        )
        return upward, downward

    for slot in range(HEADS):
        upward, downward = row_copies(slot)
        pl.when(has_next)(upward.start)
        pl.when(has_prev)(downward.start)

    def main_copies(slot):
        where = slot_device(slot)
        at_home = send(
            packed.at[slot], main.at[me + 4], main_send.at[slot], main_recv.at[me + 3],
            {"tm": ring * RING + where},
        )
        local = pltpu.make_async_copy(packed.at[slot], main.at[me + 4], main_recv.at[me + 3])
        down = send(
            packed.at[slot, 0], main.at[me + 12, 0], main_next.at[slot], main_recv.at[me + 11],
            {"tm": (ring - 1) * RING + where},
        )
        up = send(
            packed.at[slot, 0], main.at[me - 4, 0], main_next.at[slot], main_recv.at[me - 5],
            {"tm": (ring + 1) * RING + where},
        )
        return where, at_home, local, down, up

    def main_start(slot):
        where, at_home, local, down, up = main_copies(slot)
        pl.when(where != me)(lambda: at_home.start())
        pl.when(where == me)(lambda: local.start())
        pl.when(to_down)(lambda: down.start())
        pl.when(to_up)(lambda: up.start())

    for_each(HEADS, main_start)

    def clear(first, count):
        def one(i):
            main[first + i, 0] = jnp.zeros((CELL, 2 * WIDTH), BF16)
            hstage[first + i] = jnp.zeros((2 * EDGE, 2 * WIDTH), BF16)

        for_each(count, one)

    clear(0, 1)
    clear(15, 1)
    pl.when(jnp.logical_not(has_down))(lambda: clear(1, 3))
    pl.when(jnp.logical_not(has_up))(lambda: clear(12, 3))

    def clear_halo(first):
        def one(slot):
            halo[slot, pl.ds(first, EDGE)] = jnp.zeros((EDGE, 2 * WIDTH), BF16)

        for_each(HEADS, one)

    pl.when(jnp.logical_not(has_prev))(lambda: clear_halo(0))
    pl.when(jnp.logical_not(has_next))(lambda: clear_halo(EDGE))

    def clear_total(i):
        total[i] = jnp.zeros((2 * WIDTH, 2 * WIDTH), F32)

    for_each(2 * HALO + ROWS, clear_total)

    shape = (RING * COLS, SPAN * COLS)
    query_at = lax.broadcasted_iota(jnp.int32, shape, 0)
    key_at = lax.broadcasted_iota(jnp.int32, shape, 1)
    frame_apart = lax.shift_right_logical(key_at, 3) - lax.shift_right_logical(query_at, 3) - 4
    key_frame = lax.shift_right_logical(key_at, 3) + ring * RING - 4
    col_apart = (key_at & 7) - (query_at & 7)
    seen = (
        (jnp.abs(frame_apart) <= REACH)
        & (key_frame >= 0)
        & (key_frame < rings * RING)
        & (jnp.abs(col_apart) <= REACH * step)
        & ((col_apart & (step - 1)) == 0)
    )
    bias[0] = jnp.where(seen, 0.0, -1e30)
    bias[1] = jnp.full(shape, -1e30, F32)

    def halo_copies(slot):
        size = HALO_ROWS[slot] * COLS
        where = 2 * (slot % 4) + slot // 4
        part = pl.ds(EDGE - size, 2 * size)
        source = halo.at[slot, part]
        at_home = send(
            source, hstage.at[me + 4, part], halo_send.at[slot], halo_recv.at[me + 3],
            {"tm": ring * RING + where},
        )
        local = pltpu.make_async_copy(source, hstage.at[me + 4, part], halo_recv.at[me + 3])
        down = send(
            source, hstage.at[me + 12, part], halo_next.at[slot], halo_recv.at[me + 11],
            {"tm": (ring - 1) * RING + where},
        )
        up = send(
            source, hstage.at[me - 4, part], halo_next.at[slot], halo_recv.at[me - 5],
            {"tm": (ring + 1) * RING + where},
        )
        return where, at_home, local, down, up

    for slot in range(HEADS):
        upward, downward = row_copies(slot)
        pl.when(has_prev)(upward.wait_recv)
        pl.when(has_next)(downward.wait_recv)
        where, at_home, local, down, up = halo_copies(slot)
        pl.when(me != where)(at_home.start)
        pl.when(me == where)(local.start)
        pl.when(to_down)(down.start)
        pl.when(to_up)(up.start)

    def main_wait(i):
        arrived(main.at[i + 4], main_recv.at[i + 3])

    for_each(RING, main_wait)

    def main_wait_down(i):
        arrived(main.at[i + 1, 0], main_recv.at[i])

    pl.when(has_down)(lambda: for_each(3, main_wait_down))

    def main_wait_up(i):
        arrived(main.at[i + 12, 0], main_recv.at[i + 11])

    pl.when(has_up)(lambda: for_each(3, main_wait_up))

    def two_rows(part, frames):
        wide = part.astype(F32).reshape(frames, 2, COLS, 2 * WIDTH)
        return [
            wide[:, i].reshape(frames * COLS, 2 * WIDTH).astype(BF16) for i in range(2)
        ]

    def turn_main(pair):
        rows = pl.ds(pl.multiple_of(pair * 16, 16), 16)
        even, odd = two_rows(main[:, 0, rows], SPAN)
        keys[HALO + 2 * pair] = even
        keys[HALO + 2 * pair + 1] = odd
        even, odd = two_rows(main[pl.ds(4, RING), 1, rows], RING)
        quers[2 * pair] = even
        quers[2 * pair + 1] = odd

    for_each(ROWS // 2, turn_main)

    def halo_wait(rows):
        part = pl.ds(EDGE - rows * COLS, 2 * rows * COLS)

        def one(i):
            arrived(hstage.at[i + 1, part], halo_recv.at[i])

        def some(first, count):
            for_each(count, lambda i: one(first + i))

        some(3, RING)
        pl.when(has_down)(lambda: some(0, 3))
        pl.when(has_up)(lambda: some(11, 3))

    by_group(halo_wait)

    def turn_halo(pair):
        rows = pl.ds(pl.multiple_of(pair * 16, 16), 16)
        even, odd = two_rows(hstage[:, rows], SPAN)
        place = 2 * pair + jnp.where(pair < HALO // 2, 0, ROWS)
        keys[place] = even
        keys[place + 1] = odd

    for_each(HALO, turn_halo)

    low = low_lanes(RING * COLS)
    wide = SPAN * COLS
    tall = RING * COLS
    scale = WIDTH ** -0.5 * 1.4426950408889634
    for half in range(2):
        probs[pl.ds(0, tall), pl.ds(7 * wide, wide)] = jnp.zeros((tall, wide), BF16)
        probs[pl.ds(tall, tall), pl.ds(0, wide)] = jnp.zeros((tall, wide), BF16)
        probs[pl.ds(2 * tall, tall), pl.ds(7 * wide, wide)] = jnp.zeros((tall, wide), BF16)
        probs[pl.ds(3 * tall, tall), pl.ds(0, wide)] = jnp.zeros((tall, wide), BF16)

    def attend(i):
        first = lax.div(i, step) * (2 * step) + lax.rem(i, step)
        pair = [quers[first], quers[first + step]]
        none = jnp.zeros_like(pair[0])
        left = jnp.concatenate(
            [jnp.where(low, q, none) for q in pair] + [jnp.where(low, none, q) for q in pair], 0
        )
        places = [first + HALO + step * (j - REACH) for j in range(8)]
        block = jnp.concatenate([keys[place] for place in places], 0)
        scores[...] = lax.dot_general(
            left, block, (((1,), (1,)), ((), ())), preferred_element_type=F32
        )
        outside = []
        for place in places:
            row = place - HALO + space * ROWS
            outside.append(jnp.where((row < 0) | (row >= blocks * ROWS), 1, 0))
        chunk = 16
        for half in range(2):
            for start in range(0, tall, chunk):
                rows = pl.ds(half * tall + start, chunk)
                grad_rows = pl.ds((2 + half) * tall + start, chunk)
                tiles = range(half, half + 7)
                raw = [
                    scores[rows, pl.ds(j * wide, wide)]
                    + bias[outside[j], pl.ds(start, chunk)]
                    for j in tiles
                ]
                peak = jnp.max(functools.reduce(jnp.maximum, raw), axis=1, keepdims=True)
                power = [jnp.exp2((tile - peak) * scale) for tile in raw]
                gains = [scores[grad_rows, pl.ds(j * wide, wide)] for j in tiles]
                summed = jnp.sum(functools.reduce(jnp.add, power), axis=1, keepdims=True)
                inverse = 1.0 / summed
                delta = inverse * jnp.sum(
                    functools.reduce(jnp.add, [a * b for a, b in zip(power, gains)]),
                    axis=1,
                    keepdims=True,
                )
                for j, a, b in zip(tiles, power, gains):
                    weight = a * inverse
                    probs[grad_rows, pl.ds(j * wide, wide)] = weight.astype(BF16)
                    probs[rows, pl.ds(j * wide, wide)] = (weight * (b - delta)).astype(BF16)
        both = probs[...]
        out = jnp.dot(both, block, preferred_element_type=F32)
        for half in range(2):
            grad_query = out[half * tall : (half + 1) * tall] * WIDTH ** -0.5
            attended = out[(2 + half) * tall : (3 + half) * tall]
            quers[first + half * step] = jnp.where(low, grad_query, attended).astype(BF16)
        back = lax.dot_general(left, both, (((0,), (0,)), ((), ())), preferred_element_type=F32)
        for j, place in enumerate(places):
            total[place] += back[:, j * wide : (j + 1) * wide]

    for_each(ROWS // 2, attend)

    low_all = low_lanes(SPAN * COLS)

    def key_row(place):
        turned = total[place].T
        return jnp.where(low_all, turned * WIDTH ** -0.5, turned).reshape(SPAN, COLS, 2 * WIDTH)

    def back_halo(pair):
        place = 2 * pair + jnp.where(pair < HALO // 2, 0, ROWS)
        both = jnp.concatenate([key_row(place), key_row(place + 1)], 1)
        ghalo[:, pl.ds(pl.multiple_of(pair * 16, 16), 16)] = both.astype(BF16)

    for_each(HALO, back_halo)

    def ghalo_copies(rows, i):
        part = pl.ds(EDGE - rows * COLS, 2 * rows * COLS)
        source = ghalo.at[i + 1, part]
        at_home = send(
            source, rhalo.at[my_slot, part], ghalo_send.at[i], ghalo_recv.at[my_slot],
            {"tm": ring * RING + i - 3},
        )
        local = pltpu.make_async_copy(source, rhalo.at[my_slot, part], ghalo_recv.at[my_slot])
        down = send(
            source, rhalo_b.at[my_slot, part], ghalo_send.at[i], ghalo_recv_b.at[my_slot],
            {"tm": (ring - 1) * RING + i + 5},
        )
        up = send(
            source, rhalo_b.at[my_slot, part], ghalo_send.at[i], ghalo_recv_b.at[my_slot],
            {"tm": (ring + 1) * RING + i - 11},
        )
        return at_home, local, down, up

    def ghalo_start(rows):
        def at_home(i):
            pl.when(i != me)(lambda: ghalo_copies(rows, i + 3)[0].start())
            pl.when(i == me)(lambda: ghalo_copies(rows, i + 3)[1].start())

        for_each(RING, at_home)
        pl.when(has_down)(lambda: for_each(3, lambda i: ghalo_copies(rows, i)[2].start()))
        pl.when(has_up)(lambda: for_each(3, lambda i: ghalo_copies(rows, i + 11)[3].start()))

    by_group(ghalo_start)

    def back_main(pair):
        rows = pl.ds(pl.multiple_of(pair * 16, 16), 16)
        place = HALO + 2 * pair
        both = jnp.concatenate([key_row(place), key_row(place + 1)], 1)
        gmain[:, 0, rows] = both.astype(BF16)
        outs = [
            quers[2 * pair + i].astype(F32).reshape(RING, COLS, 2 * WIDTH) for i in range(2)
        ]
        gmain[pl.ds(4, RING), 1, rows] = jnp.concatenate(outs, 1).astype(BF16)

    for_each(ROWS // 2, back_main)

    def gmain_copies(i):
        at_home = send(
            gmain.at[i + 1], rmain.at[my_slot], gmain_send.at[i], gmain_recv.at[my_slot],
            {"tm": ring * RING + i - 3},
        )
        local = pltpu.make_async_copy(gmain.at[i + 1], rmain.at[my_slot], gmain_recv.at[my_slot])
        down = send(
            gmain.at[i + 1, 0], rmain_b.at[my_slot], gmain_send.at[i], gmain_recv_b.at[my_slot],
            {"tm": (ring - 1) * RING + i + 5},
        )
        up = send(
            gmain.at[i + 1, 0], rmain_b.at[my_slot], gmain_send.at[i], gmain_recv_b.at[my_slot],
            {"tm": (ring + 1) * RING + i - 11},
        )
        return at_home, local, down, up

    def gmain_start(i):
        pl.when(i != me)(lambda: gmain_copies(i + 3)[0].start())
        pl.when(i == me)(lambda: gmain_copies(i + 3)[1].start())

    for_each(RING, gmain_start)
    pl.when(has_down)(lambda: for_each(3, lambda i: gmain_copies(i)[2].start()))
    pl.when(has_up)(lambda: for_each(3, lambda i: gmain_copies(i + 11)[3].start()))

    def back_copies(slot):
        size = HALO_ROWS[slot] * COLS
        lower = pl.ds(EDGE - size, size)
        upper = pl.ds(EDGE, size)
        downward = send(
            hsum.at[slot, lower], rrow.at[slot, lower], back_send.at[slot, 0],
            back_recv.at[slot, 0], {"space": space - 1},
        )
        upward = send(
            hsum.at[slot, upper], rrow.at[slot, upper], back_send.at[slot, 1],
            back_recv.at[slot, 1], {"space": space + 1},
        )
        return downward, upward

    for slot in range(HEADS):
        size = HALO_ROWS[slot] * COLS
        part = pl.ds(EDGE - size, 2 * size)
        arrived(rhalo.at[slot, part], ghalo_recv.at[slot])

        @pl.when(shared)
        def _():
            arrived(rhalo_b.at[slot, part], ghalo_recv_b.at[slot])
            both = rhalo[slot, part].astype(F32) + rhalo_b[slot, part].astype(F32)
            hsum[slot, part] = both.astype(BF16)

        @pl.when(jnp.logical_not(shared))
        def _():
            hsum[slot, part] = rhalo[slot, part]

        downward, upward = back_copies(slot)
        pl.when(has_prev)(downward.start)
        pl.when(has_next)(upward.start)

    for slot in range(HEADS):
        size = HALO_ROWS[slot] * COLS
        arrived(rmain.at[slot], gmain_recv.at[slot])
        final[...] = rmain[slot, 0].astype(F32)

        @pl.when(shared)
        def _():
            arrived(rmain_b.at[slot], gmain_recv_b.at[slot])
            final[...] += rmain_b[slot].astype(F32)

        downward, upward = back_copies(slot)

        @pl.when(has_next)
        def _():
            downward.wait_recv()
            final[pl.ds(CELL - size, size)] += rrow[slot, pl.ds(EDGE - size, size)].astype(F32)

        @pl.when(has_prev)
        def _():
            upward.wait_recv()
            final[pl.ds(0, size)] += rrow[slot, pl.ds(EDGE, size)].astype(F32)

        result[slot, 0] = final[...].astype(BF16)
        result[slot, 1] = rmain[slot, 1]

    for slot in range(HEADS):
        upward, downward = row_copies(slot)
        pl.when(has_next)(upward.wait_send)
        pl.when(has_prev)(downward.wait_send)
        where, at_home, local, down, up = halo_copies(slot)
        pl.when(me != where)(at_home.wait_send)
        pl.when(to_down)(down.wait_send)
        pl.when(to_up)(up.wait_send)
        downward, upward = back_copies(slot)
        pl.when(has_prev)(downward.wait_send)
        pl.when(has_next)(upward.wait_send)

    def main_sent(slot):
        where, at_home, local, down, up = main_copies(slot)
        pl.when(where != me)(lambda: at_home.wait_send())
        pl.when(to_down)(lambda: down.wait_send())
        pl.when(to_up)(lambda: up.wait_send())

    for_each(HEADS, main_sent)

    def gmain_sent(i):
        pl.when(i != me)(lambda: gmain_copies(i + 3)[0].wait_send())

    for_each(RING, gmain_sent)
    pl.when(has_down)(lambda: for_each(3, lambda i: gmain_copies(i)[2].wait_send()))
    pl.when(has_up)(lambda: for_each(3, lambda i: gmain_copies(i + 11)[3].wait_send()))

    def ghalo_sent(rows):
        def at_home(i):
            pl.when(i != me)(lambda: ghalo_copies(rows, i + 3)[0].wait_send())

        for_each(RING, at_home)
        pl.when(has_down)(lambda: for_each(3, lambda i: ghalo_copies(rows, i)[2].wait_send()))
        pl.when(has_up)(lambda: for_each(3, lambda i: ghalo_copies(rows, i + 11)[3].wait_send()))

    by_group(ghalo_sent)


def shards(queries, key_vectors, values, cotangent, dilation):
    frames, rows, cols, width = queries.shape
    flat = [a.reshape(CELL, width) for a in (queries, key_vectors, values, cotangent)]
    smem = pl.BlockSpec(memory_space=pltpu.SMEM)
    vmem = pl.BlockSpec(memory_space=pltpu.VMEM)
    lanes = 2 * WIDTH
    packed = pl.pallas_call(
        pack_kernel,
        out_shape=jax.ShapeDtypeStruct((HEADS, 2, CELL, lanes), BF16),
        in_specs=[smem, vmem, vmem, vmem, vmem],
        out_specs=vmem,
        name="pack_heads",
    )(dilation, *flat)
    dma = pltpu.SemaphoreType.DMA
    result = pl.pallas_call(
        functools.partial(main_kernel, lax.axis_size("tm") // RING, lax.axis_size("space")),
        out_shape=jax.ShapeDtypeStruct((HEADS, 2, CELL, lanes), BF16),
        in_specs=[vmem],
        out_specs=vmem,
        scratch_shapes=[
            pltpu.VMEM((HEADS, 2 * EDGE, lanes), BF16),
            pltpu.VMEM((SPAN, 2, CELL, lanes), BF16),
            pltpu.VMEM((SPAN, 2 * EDGE, lanes), BF16),
            pltpu.VMEM((ROWS + 2 * HALO, SPAN * COLS, lanes), BF16),
            pltpu.VMEM((ROWS, RING * COLS, lanes), BF16),
            pltpu.VMEM((2, RING * COLS, SPAN * COLS), F32),
            pltpu.VMEM((4 * RING * COLS, 8 * SPAN * COLS), F32),
            pltpu.VMEM((4 * RING * COLS, 8 * SPAN * COLS), BF16),
            pltpu.VMEM((ROWS + 2 * HALO, lanes, SPAN * COLS), F32),
            pltpu.VMEM((SPAN, 2, CELL, lanes), BF16),
            pltpu.VMEM((SPAN, 2 * EDGE, lanes), BF16),
            pltpu.VMEM((HEADS, 2, CELL, lanes), BF16),
            pltpu.VMEM((HEADS, CELL, lanes), BF16),
            pltpu.VMEM((HEADS, 2 * EDGE, lanes), BF16),
            pltpu.VMEM((HEADS, 2 * EDGE, lanes), BF16),
            pltpu.VMEM((HEADS, 2 * EDGE, lanes), BF16),
            pltpu.VMEM((HEADS, 2 * EDGE, lanes), BF16),
            pltpu.VMEM((CELL, lanes), F32),
            dma((HEADS, 2)),
            dma((HEADS, 2)),
            dma((HEADS,)),
            dma((HEADS,)),
            dma((14,)),
            dma((HEADS,)),
            dma((HEADS,)),
            dma((14,)),
            dma((14,)),
            dma((HEADS,)),
            dma((HEADS,)),
            dma((14,)),
            dma((HEADS,)),
            dma((HEADS,)),
            dma((HEADS, 2)),
            dma((HEADS, 2)),
        ],
        compiler_params=pltpu.CompilerParams(
            collective_id=0, has_side_effects=True, vmem_limit_bytes=40 * 1024 * 1024
        ),
        name="neighbourhood_attention",
    )(packed)
    outs = pl.pallas_call(
        unpack_kernel,
        out_shape=[jax.ShapeDtypeStruct((CELL, width), BF16)] * 4,
        in_specs=[smem, vmem],
        out_specs=[vmem] * 4,
        name="unpack_heads",
    )(dilation, result)
    return tuple(a.reshape(frames, rows, cols, width) for a in outs)


def solution(mesh):
    placed = P("tm", "space", None, None)
    return jax.shard_map(
        shards,
        mesh=mesh,
        in_specs=(placed, placed, placed, placed, P()),
        out_specs=(placed, placed, placed, placed),
        check_vma=False,
    )
```

```python
import functools

import jax
import jax.numpy as jnp
from jax import lax
from jax.experimental import pallas as pl
from jax.experimental.pallas import tpu as pltpu
from jax.sharding import PartitionSpec as P

HEADS = 8
WIDTH = 64
ROWS = 16
COLS = 8
RING = 8
REACH = 3
SPAN = 16
CELL = ROWS * COLS
HALO = 12
EDGE = HALO * COLS
MESH = pl.DeviceIdType.MESH
F32 = jnp.float32
BF16 = jnp.bfloat16

HALO_ROWS = (12, 12, 12, 12, 4, 4, 6, 6)
GROUP_ROWS = (12, 4, 6)


def slot_device(slot):
    return 2 * lax.rem(slot, 4) + lax.div(slot, 4)


def head_ranks(dilation):
    steps = [dilation[h] for h in range(HEADS)]
    ranks = []
    for h in range(HEADS):
        rank = jnp.int32(0)
        for other in range(HEADS):
            before = steps[other] <= steps[h] if other < h else steps[other] < steps[h]
            if other != h:
                rank = rank + jnp.where(before, 1, 0)
        ranks.append(rank)
    return ranks


def low_lanes(rows):
    return lax.broadcasted_iota(jnp.int32, (rows, 2 * WIDTH), 1) < WIDTH


def pick(ref, chosen):
    width = 2 * WIDTH
    block = ref[:, pl.ds(0, width)]
    for number in range(1, HEADS // 2):
        here = chosen[2 * number] | chosen[2 * number + 1]
        block = jnp.where(here, ref[:, pl.ds(number * width, width)], block)
    return block.astype(F32)


def pack(dilation, first, second, packed, place):
    ranks = head_ranks(dilation)
    low = low_lanes(CELL)
    for slot in range(HEADS):
        chosen = [ranks[h] == (slot + 4) % HEADS for h in range(HEADS)]
        odd = chosen[1] | chosen[3] | chosen[5] | chosen[7]
        a = pick(first, chosen)
        b = pick(second, chosen)
        a = jnp.where(odd, pltpu.roll(a, WIDTH, 1), a)
        b = jnp.where(odd, b, pltpu.roll(b, WIDTH, 1))
        packed[slot, place] = jnp.where(low, a, b).astype(BF16)


def unpack_kernel(
    dilation_in,
    result_in,
    attended_out,
    grad_query_out,
    grad_key_out,
    grad_value_out,
    dilation,
    result,
    attended,
    grad_query,
    grad_key,
    grad_value,
    load,
    store,
):
    loads = [
        pltpu.make_async_copy(result_in.at[slot], result.at[slot], load.at[slot])
        for slot in range(HEADS)
    ]
    loads.append(pltpu.make_async_copy(dilation_in, dilation, load.at[HEADS]))
    for copy in loads:
        copy.start()
    for copy in loads:
        copy.wait()
    ranks = head_ranks(dilation)
    low = low_lanes(CELL)
    pairs = ((grad_key, grad_value), (grad_query, attended))
    outs = ((grad_key_out, grad_value_out), (grad_query_out, attended_out))
    stores = []
    for place in range(2):
        first, second = pairs[place]
        for block in range(HEADS // 2):
            slots = [lax.rem(ranks[2 * block + i] + 4, HEADS) for i in range(2)]
            lanes = pl.ds(block * 2 * WIDTH, 2 * WIDTH)
            a = result[slots[0], place].astype(F32)
            b = result[slots[1], place].astype(F32)
            first[:, lanes] = jnp.where(low, a, pltpu.roll(b, WIDTH, 1)).astype(BF16)
            second[:, lanes] = jnp.where(low, pltpu.roll(a, WIDTH, 1), b).astype(BF16)
        for i in range(2):
            copy = pltpu.make_async_copy(pairs[place][i], outs[place][i], store.at[2 * place + i])
            copy.start()
            stores.append(copy)
    for copy in stores:
        copy.wait()


def for_each(count, body):
    def step(i, carry):
        body(i)
        return carry

    lax.fori_loop(0, count, step, 0)


def main_kernel(
    rings,
    blocks,
    dilation_in,
    query_in,
    key_in,
    value_in,
    grad_in,
    output,
    dilation,
    query,
    key,
    value,
    grad,
    packed,
    main,
    hstage,
    keys,
    quers,
    bias,
    scores,
    probs,
    total,
    gmain,
    ghalo,
    cmain,
    chalo,
    rmain,
    rhalo,
    final,
    result,
    load,
    store,
    main_send,
    main_recv,
    halo_send,
    halo_recv,
    near_send,
    near_recv,
    gmain_send,
    gmain_recv,
    ghalo_send,
    ghalo_recv,
    gnear_send,
    gnear_recv,
):
    tm = lax.axis_index("tm")
    space = lax.axis_index("space")
    ring = lax.div(tm, RING)
    me = lax.rem(tm, RING)
    my_slot = lax.rem(me, 2) * 4 + lax.div(me, 2)
    group = jnp.where(lax.rem(me, 2) == 0, 0, jnp.where(me < 4, 1, 2))
    step = jnp.where(group == 0, 4, group)
    has_down = ring > 0
    has_up = ring < rings - 1
    has_prev = space > 0
    has_next = space < blocks - 1

    def by_group(body):
        for number, rows in enumerate(GROUP_ROWS):
            pl.when(group == number)(functools.partial(body, rows))

    def send(source, target, send_sem, recv_sem, where):
        return pltpu.make_async_remote_copy(
            src_ref=source,
            dst_ref=target,
            send_sem=send_sem,
            recv_sem=recv_sem,
            device_id=where,
            device_id_type=MESH,
        )

    def arrived(ref, sem):
        pltpu.make_async_copy(ref, ref, sem).wait()

    loads = [
        pltpu.make_async_copy(source, target, load.at[number])
        for number, (source, target) in enumerate(
            (
                (dilation_in, dilation),
                (key_in, key),
                (value_in, value),
                (query_in, query),
                (grad_in, grad),
            )
        )
    ]
    for copy in loads:
        copy.start()

    barrier = pltpu.get_barrier_semaphore()

    def hello(where):
        pl.semaphore_signal(barrier, inc=1, device_id=where, device_id_type=MESH)

    def greet(i):
        there = ring * RING + i
        pl.when(i != me)(lambda: hello({"tm": there}))
        pl.when(has_prev)(lambda: hello({"tm": there, "space": space - 1}))
        pl.when(has_next)(lambda: hello({"tm": there, "space": space + 1}))

    for_each(RING, greet)
    pl.when(has_down)(lambda: hello({"tm": tm - RING}))
    pl.when(has_up)(lambda: hello({"tm": tm + RING}))
    for copy in loads[:3]:
        copy.wait()
    pack(dilation, key, value, packed, 0)
    greeted = (
        RING
        - 1
        + jnp.where(has_down, 1, 0)
        + jnp.where(has_up, 1, 0)
        + jnp.where(has_prev, RING, 0)
        + jnp.where(has_next, RING, 0)
    )
    pl.semaphore_wait(barrier, greeted)

    def halo_copies(slot):
        size = HALO_ROWS[slot] * COLS
        there = ring * RING + 2 * (slot % 4) + slot // 4
        upward = send(
            packed.at[slot, 0, pl.ds(CELL - size, size)],
            hstage.at[me + 4, pl.ds(EDGE - size, size)],
            halo_send.at[slot, 0],
            halo_recv.at[me, 0],
            {"tm": there, "space": space + 1},
        )
        downward = send(
            packed.at[slot, 0, pl.ds(0, size)],
            hstage.at[me + 4, pl.ds(EDGE, size)],
            halo_send.at[slot, 1],
            halo_recv.at[me, 1],
            {"tm": there, "space": space - 1},
        )
        return upward, downward

    for slot in range(HEADS):
        upward, downward = halo_copies(slot)
        pl.when(has_next)(upward.start)
        pl.when(has_prev)(downward.start)

    for copy in loads[3:]:
        copy.wait()
    pack(dilation, query, grad, packed, 1)

    def main_copies(slot):
        where = slot_device(slot)
        at_home = send(
            packed.at[slot], main.at[me + 4], main_send.at[slot], main_recv.at[me],
            {"tm": ring * RING + where},
        )
        local = pltpu.make_async_copy(packed.at[slot], main.at[me + 4], main_recv.at[me])
        return where, at_home, local

    def main_start(slot):
        where, at_home, local = main_copies(slot)
        pl.when(where != me)(lambda: at_home.start())
        pl.when(where == me)(lambda: local.start())

    for_each(HEADS, main_start)

    def clear(first, count):
        def one(i):
            main[first + i, 0] = jnp.zeros((CELL, 2 * WIDTH), BF16)
            hstage[first + i] = jnp.zeros((2 * EDGE, 2 * WIDTH), BF16)

        for_each(count, one)

    clear(0, 1)
    clear(15, 1)
    pl.when(jnp.logical_not(has_down))(lambda: clear(1, 3))
    pl.when(jnp.logical_not(has_up))(lambda: clear(12, 3))

    def clear_halo(first):
        def one(i):
            hstage[i + 4, pl.ds(first, EDGE)] = jnp.zeros((EDGE, 2 * WIDTH), BF16)

        for_each(RING, one)

    pl.when(jnp.logical_not(has_prev))(lambda: clear_halo(0))
    pl.when(jnp.logical_not(has_next))(lambda: clear_halo(EDGE))

    def clear_total(i):
        total[i] = jnp.zeros((2 * WIDTH, 2 * WIDTH), F32)

    for_each(2 * HALO + ROWS, clear_total)

    shape = (RING * COLS, SPAN * COLS)
    query_at = lax.broadcasted_iota(jnp.int32, shape, 0)
    key_at = lax.broadcasted_iota(jnp.int32, shape, 1)
    frame_apart = lax.shift_right_logical(key_at, 3) - lax.shift_right_logical(query_at, 3) - 4
    key_frame = lax.shift_right_logical(key_at, 3) + ring * RING - 4
    col_apart = (key_at & 7) - (query_at & 7)
    seen = (
        (jnp.abs(frame_apart) <= REACH)
        & (key_frame >= 0)
        & (key_frame < rings * RING)
        & (jnp.abs(col_apart) <= REACH * step)
        & ((col_apart & (step - 1)) == 0)
    )
    bias[0] = jnp.where(seen, 0.0, -1e30)
    bias[1] = jnp.full(shape, -1e30, F32)

    def main_wait(i):
        arrived(main.at[i + 4], main_recv.at[i])

    def near_main():
        down = send(
            main.at[pl.ds(4, 3), 0], main.at[pl.ds(12, 3), 0], near_send.at[0], near_recv.at[0],
            {"tm": tm - RING},
        )
        up = send(
            main.at[pl.ds(9, 3), 0], main.at[pl.ds(1, 3), 0], near_send.at[1], near_recv.at[1],
            {"tm": tm + RING},
        )
        return down, up

    def near_halo(rows):
        part = pl.ds(EDGE - rows * COLS, 2 * rows * COLS)
        down = send(
            hstage.at[pl.ds(4, 3), part], hstage.at[pl.ds(12, 3), part],
            near_send.at[2], near_recv.at[2], {"tm": tm - RING},
        )
        up = send(
            hstage.at[pl.ds(9, 3), part], hstage.at[pl.ds(1, 3), part],
            near_send.at[3], near_recv.at[3], {"tm": tm + RING},
        )
        return down, up

    for_each(3, main_wait)
    pl.when(has_down)(lambda: near_main()[0].start())
    for_each(3, lambda i: main_wait(i + 5))
    pl.when(has_up)(lambda: near_main()[1].start())
    for_each(2, lambda i: main_wait(i + 3))

    def halo_phase(rows):
        size = rows * COLS

        def one(i):
            pl.when(has_prev)(
                lambda: arrived(hstage.at[i + 4, pl.ds(EDGE - size, size)], halo_recv.at[i, 0])
            )
            pl.when(has_next)(
                lambda: arrived(hstage.at[i + 4, pl.ds(EDGE, size)], halo_recv.at[i, 1])
            )

        for_each(3, one)
        pl.when(has_down)(lambda: near_halo(rows)[0].start())
        for_each(3, lambda i: one(i + 5))
        pl.when(has_up)(lambda: near_halo(rows)[1].start())
        for_each(2, lambda i: one(i + 3))

    by_group(halo_phase)
    pl.when(has_down)(lambda: near_main()[1].wait_recv())
    pl.when(has_up)(lambda: near_main()[0].wait_recv())

    def two_rows(part, frames):
        wide = part.astype(F32).reshape(frames, 2, COLS, 2 * WIDTH)
        return [wide[:, i].reshape(frames * COLS, 2 * WIDTH).astype(BF16) for i in range(2)]

    def turn_main(pair):
        rows = pl.ds(pl.multiple_of(pair * 16, 16), 16)
        even, odd = two_rows(main[:, 0, rows], SPAN)
        keys[HALO + 2 * pair] = even
        keys[HALO + 2 * pair + 1] = odd
        even, odd = two_rows(main[pl.ds(4, RING), 1, rows], RING)
        quers[2 * pair] = even
        quers[2 * pair + 1] = odd

    for_each(ROWS // 2, turn_main)

    def near_halo_wait(rows):
        pl.when(has_down)(lambda: near_halo(rows)[1].wait_recv())
        pl.when(has_up)(lambda: near_halo(rows)[0].wait_recv())

    by_group(near_halo_wait)

    def turn_halo(pair):
        rows = pl.ds(pl.multiple_of(pair * 16, 16), 16)
        even, odd = two_rows(hstage[:, rows], SPAN)
        place = 2 * pair + jnp.where(pair < HALO // 2, 0, ROWS)
        keys[place] = even
        keys[place + 1] = odd

    for_each(HALO, turn_halo)

    low = low_lanes(RING * COLS)
    wide = SPAN * COLS
    tall = RING * COLS
    scale = WIDTH ** -0.5 * 1.4426950408889634
    for part in range(4):
        unseen = pl.ds(0 if part % 2 else 7 * wide, wide)
        probs[pl.ds(part * tall, tall), unseen] = jnp.zeros((tall, wide), BF16)

    def attend(i):
        first = lax.div(i, step) * (2 * step) + lax.rem(i, step)
        pair = [quers[first], quers[first + step]]
        none = jnp.zeros_like(pair[0])
        left = jnp.concatenate(
            [jnp.where(low, q, none) for q in pair] + [jnp.where(low, none, q) for q in pair], 0
        )
        places = [first + HALO + step * (j - REACH) for j in range(8)]
        block = jnp.concatenate([keys[place] for place in places], 0)
        scores[...] = lax.dot_general(
            left, block, (((1,), (1,)), ((), ())), preferred_element_type=F32
        )
        outside = []
        for place in places:
            row = place - HALO + space * ROWS
            outside.append(jnp.where((row < 0) | (row >= blocks * ROWS), 1, 0))
        chunk = 16
        for half in range(2):
            for start in range(0, tall, chunk):
                rows = pl.ds(half * tall + start, chunk)
                grad_rows = pl.ds((2 + half) * tall + start, chunk)
                tiles = range(half, half + 7)
                raw = [
                    scores[rows, pl.ds(j * wide, wide)]
                    + bias[outside[j], pl.ds(start, chunk)]
                    for j in tiles
                ]
                peak = jnp.max(functools.reduce(jnp.maximum, raw), axis=1, keepdims=True)
                power = [jnp.exp2((tile - peak) * scale) for tile in raw]
                gains = [scores[grad_rows, pl.ds(j * wide, wide)] for j in tiles]
                summed = jnp.sum(functools.reduce(jnp.add, power), axis=1, keepdims=True)
                inverse = 1.0 / summed
                delta = inverse * jnp.sum(
                    functools.reduce(jnp.add, [a * b for a, b in zip(power, gains)]),
                    axis=1,
                    keepdims=True,
                )
                for j, a, b in zip(tiles, power, gains):
                    weight = a * inverse
                    probs[grad_rows, pl.ds(j * wide, wide)] = weight.astype(BF16)
                    probs[rows, pl.ds(j * wide, wide)] = (weight * (b - delta)).astype(BF16)
        both = probs[...]
        out = jnp.dot(both, block, preferred_element_type=F32)
        for half in range(2):
            grad_query = out[half * tall : (half + 1) * tall] * WIDTH ** -0.5
            attended = out[(2 + half) * tall : (3 + half) * tall]
            quers[first + half * step] = jnp.where(low, grad_query, attended).astype(BF16)
        back = lax.dot_general(left, both, (((0,), (0,)), ((), ())), preferred_element_type=F32)
        for j, place in enumerate(places):
            total[place] += back[:, j * wide : (j + 1) * wide]

    for_each(ROWS // 2, attend)

    low_all = low_lanes(SPAN * COLS)

    def key_row(place):
        turned = total[place].T
        return jnp.where(low_all, turned * WIDTH ** -0.5, turned).reshape(SPAN, COLS, 2 * WIDTH)

    def back_halo(pair):
        place = 2 * pair + jnp.where(pair < HALO // 2, 0, ROWS)
        both = jnp.concatenate([key_row(place), key_row(place + 1)], 1)
        ghalo[:, pl.ds(pl.multiple_of(pair * 16, 16), 16)] = both.astype(BF16)

    for_each(HALO, back_halo)

    def gnear_halo(rows):
        part = pl.ds(EDGE - rows * COLS, 2 * rows * COLS)
        down = send(
            ghalo.at[pl.ds(1, 3), part], chalo.at[1, :, part],
            gnear_send.at[0], gnear_recv.at[0], {"tm": tm - RING},
        )
        up = send(
            ghalo.at[pl.ds(12, 3), part], chalo.at[0, :, part],
            gnear_send.at[1], gnear_recv.at[1], {"tm": tm + RING},
        )
        return down, up

    def gnear_main():
        down = send(
            gmain.at[pl.ds(1, 3), 0], cmain.at[1], gnear_send.at[2], gnear_recv.at[2],
            {"tm": tm - RING},
        )
        up = send(
            gmain.at[pl.ds(12, 3), 0], cmain.at[0], gnear_send.at[3], gnear_recv.at[3],
            {"tm": tm + RING},
        )
        return down, up

    def gnear_halo_start(rows):
        pl.when(has_down)(lambda: gnear_halo(rows)[0].start())
        pl.when(has_up)(lambda: gnear_halo(rows)[1].start())

    by_group(gnear_halo_start)

    def back_main(pair):
        rows = pl.ds(pl.multiple_of(pair * 16, 16), 16)
        place = HALO + 2 * pair
        both = jnp.concatenate([key_row(place), key_row(place + 1)], 1)
        gmain[:, 0, rows] = both.astype(BF16)
        outs = [quers[2 * pair + i].astype(F32).reshape(RING, COLS, 2 * WIDTH) for i in range(2)]
        gmain[pl.ds(4, RING), 1, rows] = jnp.concatenate(outs, 1).astype(BF16)

    for_each(ROWS // 2, back_main)
    pl.when(has_down)(lambda: gnear_main()[0].start())
    pl.when(has_up)(lambda: gnear_main()[1].start())

    def ghalo_copies(rows, i):
        size = rows * COLS
        lower = pl.ds(EDGE - size, size)
        upper = pl.ds(EDGE, size)
        there = ring * RING + i
        downward = send(
            ghalo.at[i + 4, lower], rhalo.at[my_slot, lower], ghalo_send.at[i, 0],
            ghalo_recv.at[my_slot, 0], {"tm": there, "space": space - 1},
        )
        upward = send(
            ghalo.at[i + 4, upper], rhalo.at[my_slot, upper], ghalo_send.at[i, 1],
            ghalo_recv.at[my_slot, 1], {"tm": there, "space": space + 1},
        )
        return downward, upward

    def add_halo(rows):
        part = pl.ds(EDGE - rows * COLS, 2 * rows * COLS)

        def add(first, side):
            def one(i):
                both = ghalo[first + i, part].astype(F32) + chalo[side, i, part].astype(F32)
                ghalo[first + i, part] = both.astype(BF16)

            for_each(3, one)

        def start(i):
            pl.when(has_prev)(lambda: ghalo_copies(rows, i)[0].start())
            pl.when(has_next)(lambda: ghalo_copies(rows, i)[1].start())

        for_each(2, lambda i: start(i + 3))

        @pl.when(has_down)
        def _():
            gnear_halo(rows)[1].wait_recv()
            add(4, 0)

        for_each(3, start)

        @pl.when(has_up)
        def _():
            gnear_halo(rows)[0].wait_recv()
            add(9, 1)

        for_each(3, lambda i: start(i + 5))

    by_group(add_halo)

    def gmain_copies(i):
        at_home = send(
            gmain.at[i + 4], rmain.at[my_slot], gmain_send.at[i], gmain_recv.at[my_slot],
            {"tm": ring * RING + i},
        )
        local = pltpu.make_async_copy(gmain.at[i + 4], rmain.at[my_slot], gmain_recv.at[my_slot])
        return at_home, local

    def gmain_start(i):
        pl.when(i != me)(lambda: gmain_copies(i)[0].start())
        pl.when(i == me)(lambda: gmain_copies(i)[1].start())

    def add_main(first, side):
        def one(i):
            both = gmain[first + i, 0].astype(F32) + cmain[side, i].astype(F32)
            gmain[first + i, 0] = both.astype(BF16)

        for_each(3, one)

    for_each(2, lambda i: gmain_start(i + 3))

    @pl.when(has_down)
    def _():
        gnear_main()[1].wait_recv()
        add_main(4, 0)

    for_each(3, gmain_start)

    @pl.when(has_up)
    def _():
        gnear_main()[0].wait_recv()
        add_main(9, 1)

    for_each(3, lambda i: gmain_start(i + 5))

    for slot in range(HEADS):
        size = HALO_ROWS[slot] * COLS
        lower = pl.ds(EDGE - size, size)
        upper = pl.ds(EDGE, size)
        arrived(rmain.at[slot], gmain_recv.at[slot])
        final[...] = rmain[slot, 0].astype(F32)

        @pl.when(has_next)
        def _():
            arrived(rhalo.at[slot, lower], ghalo_recv.at[slot, 0])
            final[pl.ds(CELL - size, size)] += rhalo[slot, lower].astype(F32)

        @pl.when(has_prev)
        def _():
            arrived(rhalo.at[slot, upper], ghalo_recv.at[slot, 1])
            final[pl.ds(0, size)] += rhalo[slot, upper].astype(F32)

        result[slot, 0] = final[...].astype(BF16)
        result[slot, 1] = rmain[slot, 1]
        pltpu.make_async_copy(result.at[slot], output.at[slot], store.at[slot]).start()

    for slot in range(HEADS):
        upward, downward = halo_copies(slot)
        pl.when(has_next)(upward.wait_send)
        pl.when(has_prev)(downward.wait_send)

    def main_sent(slot):
        where, at_home, local = main_copies(slot)
        pl.when(where != me)(lambda: at_home.wait_send())

    for_each(HEADS, main_sent)

    def gmain_sent(i):
        pl.when(i != me)(lambda: gmain_copies(i)[0].wait_send())

    for_each(RING, gmain_sent)

    def edges_sent(rows):
        def one(i):
            pl.when(has_prev)(lambda: ghalo_copies(rows, i)[0].wait_send())
            pl.when(has_next)(lambda: ghalo_copies(rows, i)[1].wait_send())

        for_each(RING, one)
        for number, there in enumerate((has_down, has_up)):
            pl.when(there)(lambda: near_main()[number].wait_send())
            pl.when(there)(lambda: near_halo(rows)[number].wait_send())
            pl.when(there)(lambda: gnear_halo(rows)[number].wait_send())
            pl.when(there)(lambda: gnear_main()[number].wait_send())

    by_group(edges_sent)
    for slot in range(HEADS):
        pltpu.make_async_copy(result.at[slot], output.at[slot], store.at[slot]).wait()


def shards(queries, key_vectors, values, cotangent, dilation):
    frames, rows, cols, width = queries.shape
    flat = [a.reshape(CELL, width) for a in (queries, key_vectors, values, cotangent)]
    lanes = 2 * WIDTH
    dma = pltpu.SemaphoreType.DMA
    hbm = pl.BlockSpec(memory_space=pl.ANY)
    result = pl.pallas_call(
        functools.partial(main_kernel, lax.axis_size("tm") // RING, lax.axis_size("space")),
        out_shape=jax.ShapeDtypeStruct((HEADS, 2, CELL, lanes), BF16),
        in_specs=[hbm] * 5,
        out_specs=hbm,
        scratch_shapes=[
            pltpu.SMEM((HEADS,), jnp.int32),
        ]
        + [pltpu.VMEM((CELL, width), BF16)] * 4
        + [
            pltpu.VMEM((HEADS, 2, CELL, lanes), BF16),
            pltpu.VMEM((SPAN, 2, CELL, lanes), BF16),
            pltpu.VMEM((SPAN, 2 * EDGE, lanes), BF16),
            pltpu.VMEM((ROWS + 2 * HALO, SPAN * COLS, lanes), BF16),
            pltpu.VMEM((ROWS, RING * COLS, lanes), BF16),
            pltpu.VMEM((2, RING * COLS, SPAN * COLS), F32),
            pltpu.VMEM((4 * RING * COLS, 8 * SPAN * COLS), F32),
            pltpu.VMEM((4 * RING * COLS, 8 * SPAN * COLS), BF16),
            pltpu.VMEM((ROWS + 2 * HALO, lanes, SPAN * COLS), F32),
            pltpu.VMEM((SPAN, 2, CELL, lanes), BF16),
            pltpu.VMEM((SPAN, 2 * EDGE, lanes), BF16),
            pltpu.VMEM((2, REACH, CELL, lanes), BF16),
            pltpu.VMEM((2, REACH, 2 * EDGE, lanes), BF16),
            pltpu.VMEM((HEADS, 2, CELL, lanes), BF16),
            pltpu.VMEM((HEADS, 2 * EDGE, lanes), BF16),
            pltpu.VMEM((CELL, lanes), F32),
            pltpu.VMEM((HEADS, 2, CELL, lanes), BF16),
            dma((5,)),
            dma((HEADS,)),
            dma((HEADS,)),
            dma((RING,)),
            dma((HEADS, 2)),
            dma((RING, 2)),
            dma((4,)),
            dma((4,)),
            dma((RING,)),
            dma((HEADS,)),
            dma((RING, 2)),
            dma((HEADS, 2)),
            dma((4,)),
            dma((4,)),
        ],
        compiler_params=pltpu.CompilerParams(
            collective_id=0, has_side_effects=True, vmem_limit_bytes=56 * 1024 * 1024
        ),
        name="neighbourhood_attention",
    )(dilation, *flat)
    outs = pl.pallas_call(
        unpack_kernel,
        out_shape=[jax.ShapeDtypeStruct((CELL, width), BF16)] * 4,
        in_specs=[hbm] * 2,
        out_specs=[hbm] * 4,
        scratch_shapes=[
            pltpu.SMEM((HEADS,), jnp.int32),
            pltpu.VMEM((HEADS, 2, CELL, lanes), BF16),
        ]
        + [pltpu.VMEM((CELL, width), BF16)] * 4
        + [dma((HEADS + 1,)), dma((4,))],
        compiler_params=pltpu.CompilerParams(vmem_limit_bytes=56 * 1024 * 1024),
        name="unpack_heads",
    )(dilation, result)
    return tuple(a.reshape(frames, rows, cols, width) for a in outs)


def solution(mesh):
    placed = P("tm", "space", None, None)
    return jax.shard_map(
        shards,
        mesh=mesh,
        in_specs=(placed, placed, placed, placed, P()),
        out_specs=(placed, placed, placed, placed),
        check_vma=False,
    )
```

```python
import functools

import jax
import jax.numpy as jnp
from jax import lax
from jax.experimental import pallas as pl
from jax.experimental.pallas import tpu as pltpu
from jax.sharding import PartitionSpec as P

HEADS = 8
WIDTH = 64
ROWS = 16
COLS = 8
RING = 8
REACH = 3
SPAN = 16
CELL = ROWS * COLS
HALO = 12
EDGE = HALO * COLS
MESH = pl.DeviceIdType.MESH
F32 = jnp.float32
BF16 = jnp.bfloat16

HALO_ROWS = (12, 12, 12, 12, 4, 4, 6, 6)
GROUP_ROWS = (12, 4, 6)
FAR = 4


def own_place(pair, far):
    return jnp.where(far, lax.rem(pair, 2) * 4 + lax.div(pair, 2), pair)


def edge_place(pair, far):
    return jnp.where(far, lax.rem(pair, 2) * 6 + lax.div(pair, 2), pair)


def edge_parts(rows, half):
    if rows == HALO:
        return pl.ds(half * EDGE, EDGE // 2), pl.ds(half * EDGE + EDGE // 2, EDGE // 2), pl.ds(half * EDGE, EDGE)
    size = rows * COLS
    return pl.ds(EDGE - size, size), pl.ds(EDGE, size), pl.ds(EDGE - size, 2 * size)


def own_parts(rows, half):
    if rows == HALO:
        return pl.ds(half * CELL // 2 + 16, EDGE // 2), pl.ds(half * CELL // 2, EDGE // 2)
    size = rows * COLS
    return pl.ds(CELL - size, size), pl.ds(0, size)


def slot_device(slot):
    return 2 * lax.rem(slot, 4) + lax.div(slot, 4)


def head_ranks(dilation):
    steps = [dilation[h] for h in range(HEADS)]
    ranks = []
    for h in range(HEADS):
        rank = jnp.int32(0)
        for other in range(HEADS):
            before = steps[other] <= steps[h] if other < h else steps[other] < steps[h]
            if other != h:
                rank = rank + jnp.where(before, 1, 0)
        ranks.append(rank)
    return ranks


def low_lanes(rows):
    return lax.broadcasted_iota(jnp.int32, (rows, 2 * WIDTH), 1) < WIDTH


def pick(ref, chosen):
    width = 2 * WIDTH
    block = ref[:, pl.ds(0, width)]
    for number in range(1, HEADS // 2):
        here = chosen[2 * number] | chosen[2 * number + 1]
        block = jnp.where(here, ref[:, pl.ds(number * width, width)], block)
    return block.astype(F32)


def pack(dilation, first, second, packed, place):
    ranks = head_ranks(dilation)
    low = low_lanes(CELL)
    for slot in range(HEADS):
        chosen = [ranks[h] == (slot + 4) % HEADS for h in range(HEADS)]
        odd = chosen[1] | chosen[3] | chosen[5] | chosen[7]
        a = pick(first, chosen)
        b = pick(second, chosen)
        a = jnp.where(odd, pltpu.roll(a, WIDTH, 1), a)
        b = jnp.where(odd, b, pltpu.roll(b, WIDTH, 1))
        block = jnp.where(low, a, b).astype(BF16)
        if place == 0 and slot < FAR:
            for pair in range(ROWS // 2):
                target = ((pair % 2) * 4 + pair // 2) * 16
                packed[slot, place, pl.ds(target, 16)] = block[pair * 16 : pair * 16 + 16]
        else:
            packed[slot, place] = block


def unpack_kernel(
    dilation_in,
    result_in,
    attended_out,
    grad_query_out,
    grad_key_out,
    grad_value_out,
    dilation,
    result,
    attended,
    grad_query,
    grad_key,
    grad_value,
    load,
    store,
):
    loads = [
        pltpu.make_async_copy(result_in.at[slot], result.at[slot], load.at[slot])
        for slot in range(HEADS)
    ]
    loads.append(pltpu.make_async_copy(dilation_in, dilation, load.at[HEADS]))
    for copy in loads:
        copy.start()
    for copy in loads:
        copy.wait()
    ranks = head_ranks(dilation)
    low = low_lanes(CELL)
    pairs = ((grad_key, grad_value), (grad_query, attended))
    outs = ((grad_key_out, grad_value_out), (grad_query_out, attended_out))
    stores = []
    for place in range(2):
        first, second = pairs[place]
        for block in range(HEADS // 2):
            slots = [lax.rem(ranks[2 * block + i] + 4, HEADS) for i in range(2)]
            lanes = pl.ds(block * 2 * WIDTH, 2 * WIDTH)
            a = result[slots[0], place].astype(F32)
            b = result[slots[1], place].astype(F32)
            first[:, lanes] = jnp.where(low, a, pltpu.roll(b, WIDTH, 1)).astype(BF16)
            second[:, lanes] = jnp.where(low, pltpu.roll(a, WIDTH, 1), b).astype(BF16)
        for i in range(2):
            copy = pltpu.make_async_copy(pairs[place][i], outs[place][i], store.at[2 * place + i])
            copy.start()
            stores.append(copy)
    for copy in stores:
        copy.wait()


def for_each(count, body, unroll=1):
    def step(i, carry):
        for k in range(unroll):
            body(i * unroll + k)
        return carry

    lax.fori_loop(0, count // unroll, step, 0)


def main_kernel(
    rings,
    blocks,
    dilation_in,
    query_in,
    key_in,
    value_in,
    grad_in,
    output,
    dilation,
    query,
    key,
    value,
    grad,
    packed,
    main,
    hstage,
    keys,
    quers,
    bias,
    scores,
    probs,
    total,
    gmain,
    ghalo,
    cmain,
    chalo,
    rmain,
    rhalo,
    final,
    result,
    load,
    store,
    main_send,
    main_recv,
    halo_send,
    halo_recv,
    near_send,
    near_recv,
    gmain_send,
    gmain_recv,
    ghalo_send,
    ghalo_recv,
    gnear_send,
    gnear_recv,
):
    tm = lax.axis_index("tm")
    space = lax.axis_index("space")
    ring = lax.div(tm, RING)
    me = lax.rem(tm, RING)
    my_slot = lax.rem(me, 2) * 4 + lax.div(me, 2)
    group = jnp.where(lax.rem(me, 2) == 0, 0, jnp.where(me < 4, 1, 2))
    far = group == 0
    step = jnp.where(far, 4, group)
    has_down = ring > 0
    has_up = ring < rings - 1
    has_prev = space > 0
    has_next = space < blocks - 1

    def by_group(body):
        for number, rows in enumerate(GROUP_ROWS):
            pl.when(group == number)(functools.partial(body, rows))

    def send(source, target, send_sem, recv_sem, where):
        return pltpu.make_async_remote_copy(
            src_ref=source,
            dst_ref=target,
            send_sem=send_sem,
            recv_sem=recv_sem,
            device_id=where,
            device_id_type=MESH,
        )

    def arrived(ref, sem):
        pltpu.make_async_copy(ref, ref, sem).wait()

    loads = [
        pltpu.make_async_copy(source, target, load.at[number])
        for number, (source, target) in enumerate(
            (
                (dilation_in, dilation),
                (key_in, key),
                (value_in, value),
                (query_in, query),
                (grad_in, grad),
            )
        )
    ]
    for copy in loads:
        copy.start()

    barrier = pltpu.get_barrier_semaphore()

    def hello(where):
        pl.semaphore_signal(barrier, inc=1, device_id=where, device_id_type=MESH)

    def greet(i):
        there = ring * RING + i
        pl.when(i != me)(lambda: hello({"tm": there}))
        pl.when(has_prev)(lambda: hello({"tm": there, "space": space - 1}))
        pl.when(has_next)(lambda: hello({"tm": there, "space": space + 1}))

    for_each(RING, greet)
    pl.when(has_down)(lambda: hello({"tm": tm - RING}))
    pl.when(has_up)(lambda: hello({"tm": tm + RING}))
    for copy in loads[:3]:
        copy.wait()
    pack(dilation, key, value, packed, 0)
    greeted = (
        RING
        - 1
        + jnp.where(has_down, 1, 0)
        + jnp.where(has_up, 1, 0)
        + jnp.where(has_prev, RING, 0)
        + jnp.where(has_next, RING, 0)
    )
    pl.semaphore_wait(barrier, greeted)

    def halo_copies(slot, half):
        top, bottom = own_parts(HALO_ROWS[slot], half)
        lower, upper, _ = edge_parts(HALO_ROWS[slot], half)
        there = ring * RING + 2 * (slot % 4) + slot // 4
        upward = send(
            packed.at[slot, 0, top],
            hstage.at[me + 4, lower],
            halo_send.at[slot, 0, half],
            halo_recv.at[me, 0, half],
            {"tm": there, "space": space + 1},
        )
        downward = send(
            packed.at[slot, 0, bottom],
            hstage.at[me + 4, upper],
            halo_send.at[slot, 1, half],
            halo_recv.at[me, 1, half],
            {"tm": there, "space": space - 1},
        )
        return upward, downward

    def halo_start(slot, half):
        upward, downward = halo_copies(slot, half)
        pl.when(has_next)(upward.start)
        pl.when(has_prev)(downward.start)

    for slot in (4, 5, 6, 7, 0, 1, 2, 3):
        halo_start(slot, 0)

    for copy in loads[3:]:
        copy.wait()
    pack(dilation, query, grad, packed, 1)

    def main_copies(slot):
        where = slot_device(slot)
        at_home = send(
            packed.at[slot], main.at[me + 4], main_send.at[slot], main_recv.at[me],
            {"tm": ring * RING + where},
        )
        local = pltpu.make_async_copy(packed.at[slot], main.at[me + 4], main_recv.at[me])
        return where, at_home, local

    def main_start(slot):
        where, at_home, local = main_copies(slot)
        pl.when(where != me)(lambda: at_home.start())
        pl.when(where == me)(lambda: local.start())

    for_each(HEADS, main_start)

    def clear(first, count):
        def one(i):
            main[first + i, 0] = jnp.zeros((CELL, 2 * WIDTH), BF16)
            hstage[first + i] = jnp.zeros((2 * EDGE, 2 * WIDTH), BF16)

        for_each(count, one)

    clear(0, 1)
    clear(15, 1)
    pl.when(jnp.logical_not(has_down))(lambda: clear(1, 3))
    pl.when(jnp.logical_not(has_up))(lambda: clear(12, 3))

    def clear_halo(rows):
        halves = range(2) if rows == HALO else range(1)

        def one(i):
            for half in halves:
                for number, missing in enumerate((has_prev, has_next)):
                    part = edge_parts(rows, half)[number]

                    @pl.when(jnp.logical_not(missing))
                    def _():
                        hstage[i + 4, part] = jnp.zeros((part.size, 2 * WIDTH), BF16)

        for_each(RING, one)

    by_group(clear_halo)

    def clear_total(i):
        total[i] = jnp.zeros((2 * WIDTH, 2 * WIDTH), F32)

    for_each(2 * HALO + ROWS, clear_total)

    shape = (RING * COLS, SPAN * COLS)
    query_at = lax.broadcasted_iota(jnp.int32, shape, 0)
    key_at = lax.broadcasted_iota(jnp.int32, shape, 1)
    frame_apart = lax.shift_right_logical(key_at, 3) - lax.shift_right_logical(query_at, 3) - 4
    key_frame = lax.shift_right_logical(key_at, 3) + ring * RING - 4
    col_apart = (key_at & 7) - (query_at & 7)
    seen = (
        (jnp.abs(frame_apart) <= REACH)
        & (key_frame >= 0)
        & (key_frame < rings * RING)
        & (jnp.abs(col_apart) <= REACH * step)
        & ((col_apart & (step - 1)) == 0)
    )
    bias[0] = jnp.where(seen, 0.0, -1e30)
    bias[1] = jnp.full(shape, -1e30, F32)

    def main_wait(i):
        arrived(main.at[i + 4], main_recv.at[i])

    def near_main():
        down = send(
            main.at[pl.ds(4, 3), 0], main.at[pl.ds(12, 3), 0], near_send.at[0], near_recv.at[0],
            {"tm": tm - RING},
        )
        up = send(
            main.at[pl.ds(9, 3), 0], main.at[pl.ds(1, 3), 0], near_send.at[1], near_recv.at[1],
            {"tm": tm + RING},
        )
        return down, up

    def near_halo(rows, half):
        part = edge_parts(rows, half)[2]
        down = send(
            hstage.at[pl.ds(4, 3), part], hstage.at[pl.ds(12, 3), part],
            near_send.at[2 + 2 * half], near_recv.at[2 + 2 * half], {"tm": tm - RING},
        )
        up = send(
            hstage.at[pl.ds(9, 3), part], hstage.at[pl.ds(1, 3), part],
            near_send.at[3 + 2 * half], near_recv.at[3 + 2 * half], {"tm": tm + RING},
        )
        return down, up

    for_each(3, main_wait)
    pl.when(has_down)(lambda: near_main()[0].start())
    for_each(3, lambda i: main_wait(i + 5))
    pl.when(has_up)(lambda: near_main()[1].start())
    for_each(2, lambda i: main_wait(i + 3))
    for slot in range(FAR):
        halo_start(slot, 1)


    def halo_phase(half, rows):
        lower, upper, _ = edge_parts(rows, half)

        def one(i):
            pl.when(has_prev)(lambda: arrived(hstage.at[i + 4, lower], halo_recv.at[i, 0, half]))
            pl.when(has_next)(lambda: arrived(hstage.at[i + 4, upper], halo_recv.at[i, 1, half]))

        for_each(3, one)
        pl.when(has_down)(lambda: near_halo(rows, half)[0].start())
        for_each(3, lambda i: one(i + 5))
        pl.when(has_up)(lambda: near_halo(rows, half)[1].start())
        for_each(2, lambda i: one(i + 3))

    by_group(functools.partial(halo_phase, 0))
    pl.when(has_down)(lambda: near_main()[1].wait_recv())
    pl.when(has_up)(lambda: near_main()[0].wait_recv())

    def two_rows(part, frames):
        wide = part.astype(F32).reshape(frames, 2, COLS, 2 * WIDTH)
        return [wide[:, i].reshape(frames * COLS, 2 * WIDTH).astype(BF16) for i in range(2)]

    def turn_main(pair):
        place = pl.ds(pl.multiple_of(own_place(pair, far) * 16, 16), 16)
        even, odd = two_rows(main[:, 0, place], SPAN)
        keys[HALO + 2 * pair] = even
        keys[HALO + 2 * pair + 1] = odd
        rows = pl.ds(pl.multiple_of(pair * 16, 16), 16)
        even, odd = two_rows(main[pl.ds(4, RING), 1, rows], RING)
        quers[2 * pair] = even
        quers[2 * pair + 1] = odd

    for_each(ROWS // 2, turn_main, 4)

    def near_halo_wait(half, rows):
        pl.when(has_down)(lambda: near_halo(rows, half)[1].wait_recv())
        pl.when(has_up)(lambda: near_halo(rows, half)[0].wait_recv())

    def turn_halo(pair):
        rows = pl.ds(pl.multiple_of(edge_place(pair, far) * 16, 16), 16)
        even, odd = two_rows(hstage[:, rows], SPAN)
        place = 2 * pair + jnp.where(pair < HALO // 2, 0, ROWS)
        keys[place] = even
        keys[place + 1] = odd

    by_group(functools.partial(near_halo_wait, 0))
    pl.when(far)(lambda: for_each(HALO // 2, lambda i: turn_halo(2 * i), 3))
    pl.when(jnp.logical_not(far))(lambda: for_each(HALO, turn_halo, 3))

    low = low_lanes(RING * COLS)
    wide = SPAN * COLS
    tall = RING * COLS
    scale = WIDTH ** -0.5 * 1.4426950408889634
    for part in range(4):
        unseen = pl.ds(0 if part % 2 else 7 * wide, wide)
        for lane in range(2):
            probs[lane, pl.ds(part * tall, tall), unseen] = jnp.zeros((tall, wide), BF16)

    def score(lane, first):
        pair = [quers[first], quers[first + step]]
        none = jnp.zeros_like(pair[0])
        left = jnp.concatenate(
            [jnp.where(low, q, none) for q in pair] + [jnp.where(low, none, q) for q in pair], 0
        )
        places = [first + HALO + step * (j - REACH) for j in range(8)]
        block = jnp.concatenate([keys[place] for place in places], 0)
        scores[lane] = lax.dot_general(
            left, block, (((1,), (1,)), ((), ())), preferred_element_type=F32
        )
        return left, places, block

    def soften(lane, places):
        outside = []
        for place in places:
            row = place - HALO + space * ROWS
            outside.append(jnp.where((row < 0) | (row >= blocks * ROWS), 1, 0))
        chunk = 16
        for half in range(2):
            for start in range(0, tall, chunk):
                rows = pl.ds(half * tall + start, chunk)
                grad_rows = pl.ds((2 + half) * tall + start, chunk)
                tiles = range(half, half + 7)
                raw = [
                    scores[lane, rows, pl.ds(j * wide, wide)]
                    + bias[outside[j], pl.ds(start, chunk)]
                    for j in tiles
                ]
                peak = jnp.max(functools.reduce(jnp.maximum, raw), axis=1, keepdims=True)
                power = [jnp.exp2((tile - peak) * scale) for tile in raw]
                gains = [scores[lane, grad_rows, pl.ds(j * wide, wide)] for j in tiles]
                summed = jnp.sum(functools.reduce(jnp.add, power), axis=1, keepdims=True)
                inverse = 1.0 / summed
                delta = inverse * jnp.sum(
                    functools.reduce(jnp.add, [a * b for a, b in zip(power, gains)]),
                    axis=1,
                    keepdims=True,
                )
                for j, a, b in zip(tiles, power, gains):
                    weight = a * inverse
                    probs[lane, grad_rows, pl.ds(j * wide, wide)] = weight.astype(BF16)
                    probs[lane, rows, pl.ds(j * wide, wide)] = (weight * (b - delta)).astype(BF16)

    def gather(lane, first, left, places, block):
        both = probs[lane]
        out = jnp.dot(both, block, preferred_element_type=F32)
        for half in range(2):
            grad_query = out[half * tall : (half + 1) * tall] * WIDTH ** -0.5
            attended = out[(2 + half) * tall : (3 + half) * tall]
            quers[first + half * step] = jnp.where(low, grad_query, attended).astype(BF16)
        back = lax.dot_general(left, both, (((0,), (0,)), ((), ())), preferred_element_type=F32)
        for j, place in enumerate(places):
            total[place] += back[:, j * wide : (j + 1) * wide]

    def attend(turn):
        firsts = []
        for lane in range(2):
            near = 2 * turn + lane
            apart = lax.rem(turn, 2) * 4 + lane + 2 * lax.div(turn, 2)
            i = jnp.where(far, apart, near)
            firsts.append(lax.div(i, step) * (2 * step) + lax.rem(i, step))
        scored = [score(lane, firsts[lane]) for lane in range(2)]
        for lane in range(2):
            soften(lane, scored[lane][1])
            gather(lane, firsts[lane], *scored[lane])

    low_all = low_lanes(SPAN * COLS)

    def key_row(place):
        turned = total[place].T
        return jnp.where(low_all, turned * WIDTH ** -0.5, turned).reshape(SPAN, COLS, 2 * WIDTH)

    def back_halo(pair):
        place = 2 * pair + jnp.where(pair < HALO // 2, 0, ROWS)
        both = jnp.concatenate([key_row(place), key_row(place + 1)], 1)
        ghalo[:, pl.ds(pl.multiple_of(edge_place(pair, far) * 16, 16), 16)] = both.astype(BF16)

    def gnear_halo(rows, half):
        part = edge_parts(rows, half)[2]
        down = send(
            ghalo.at[pl.ds(1, 3), part], chalo.at[1, :, part],
            gnear_send.at[2 + 2 * half], gnear_recv.at[2 + 2 * half], {"tm": tm - RING},
        )
        up = send(
            ghalo.at[pl.ds(12, 3), part], chalo.at[0, :, part],
            gnear_send.at[3 + 2 * half], gnear_recv.at[3 + 2 * half], {"tm": tm + RING},
        )
        return down, up

    def gnear_main():
        down = send(
            gmain.at[pl.ds(1, 3), 0], cmain.at[1], gnear_send.at[0], gnear_recv.at[0],
            {"tm": tm - RING},
        )
        up = send(
            gmain.at[pl.ds(12, 3), 0], cmain.at[0], gnear_send.at[1], gnear_recv.at[1],
            {"tm": tm + RING},
        )
        return down, up

    def gnear_start(half, rows):
        pl.when(has_down)(lambda: gnear_halo(rows, half)[0].start())
        pl.when(has_up)(lambda: gnear_halo(rows, half)[1].start())

    def back_main(pair):
        rows = pl.ds(pl.multiple_of(pair * 16, 16), 16)
        place = HALO + 2 * pair
        both = jnp.concatenate([key_row(place), key_row(place + 1)], 1)
        gmain[:, 0, pl.ds(pl.multiple_of(own_place(pair, far) * 16, 16), 16)] = both.astype(BF16)
        outs = [quers[2 * pair + i].astype(F32).reshape(RING, COLS, 2 * WIDTH) for i in range(2)]
        gmain[pl.ds(4, RING), 1, rows] = jnp.concatenate(outs, 1).astype(BF16)

    def ghalo_copies(rows, half, i):
        lower, upper, _ = edge_parts(rows, half)
        there = ring * RING + i
        downward = send(
            ghalo.at[i + 4, lower], rhalo.at[my_slot, lower], ghalo_send.at[i, 0, half],
            ghalo_recv.at[my_slot, 0, half], {"tm": there, "space": space - 1},
        )
        upward = send(
            ghalo.at[i + 4, upper], rhalo.at[my_slot, upper], ghalo_send.at[i, 1, half],
            ghalo_recv.at[my_slot, 1, half], {"tm": there, "space": space + 1},
        )
        return downward, upward

    def ghalo_start(half, rows, i):
        pl.when(has_prev)(lambda: ghalo_copies(rows, half, i)[0].start())
        pl.when(has_next)(lambda: ghalo_copies(rows, half, i)[1].start())

    def add_halo(half, rows):
        part = edge_parts(rows, half)[2]

        def add(first, side):
            def one(i):
                both = ghalo[first + i, part].astype(F32) + chalo[side, i, part].astype(F32)
                ghalo[first + i, part] = both.astype(BF16)

            for_each(3, one)

        for_each(2, lambda i: ghalo_start(half, rows, i + 3))

        @pl.when(has_down)
        def _():
            gnear_halo(rows, half)[1].wait_recv()
            add(4, 0)

        for_each(3, lambda i: ghalo_start(half, rows, i))

        @pl.when(has_up)
        def _():
            gnear_halo(rows, half)[0].wait_recv()
            add(9, 1)

        for_each(3, lambda i: ghalo_start(half, rows, i + 5))

    def advance(turn):
        @pl.when(far & (turn == 2))
        def _():
            near_halo_wait(1, HALO)
            for_each(HALO // 2, lambda i: turn_halo(2 * i + 1), 3)

        attend(turn)

        @pl.when(far & (turn == 0))
        def _():
            halo_phase(1, HALO)

        @pl.when(far & (turn == 1))
        def _():
            for_each(HALO // 2, lambda i: back_halo(2 * i), 3)
            gnear_start(0, HALO)

        @pl.when(far & (turn == 2))
        def _():
            add_halo(0, HALO)

    for_each(4, advance)

    pl.when(far)(lambda: for_each(HALO // 2, lambda i: back_halo(2 * i + 1), 3))
    pl.when(jnp.logical_not(far))(lambda: for_each(HALO, back_halo, 3))
    by_group(functools.partial(gnear_start, 1))
    for_each(ROWS // 2, back_main, 4)
    pl.when(has_down)(lambda: gnear_main()[0].start())
    pl.when(has_up)(lambda: gnear_main()[1].start())
    by_group(functools.partial(add_halo, 1))

    def gmain_copies(i):
        at_home = send(
            gmain.at[i + 4], rmain.at[my_slot], gmain_send.at[i], gmain_recv.at[my_slot],
            {"tm": ring * RING + i},
        )
        local = pltpu.make_async_copy(gmain.at[i + 4], rmain.at[my_slot], gmain_recv.at[my_slot])
        return at_home, local

    def gmain_start(i):
        pl.when(i != me)(lambda: gmain_copies(i)[0].start())
        pl.when(i == me)(lambda: gmain_copies(i)[1].start())

    def add_main(first, side):
        def one(i):
            both = gmain[first + i, 0].astype(F32) + cmain[side, i].astype(F32)
            gmain[first + i, 0] = both.astype(BF16)

        for_each(3, one)

    for_each(2, lambda i: gmain_start(i + 3))

    @pl.when(has_down)
    def _():
        gnear_main()[1].wait_recv()
        add_main(4, 0)

    for_each(3, gmain_start)

    @pl.when(has_up)
    def _():
        gnear_main()[0].wait_recv()
        add_main(9, 1)

    for_each(3, lambda i: gmain_start(i + 5))

    for slot in (4, 5, 6, 7, 0, 1, 2, 3):
        rows = HALO_ROWS[slot]
        arrived(rmain.at[slot], gmain_recv.at[slot])
        if slot < FAR:
            for pair in range(ROWS // 2):
                source = ((pair % 2) * 4 + pair // 2) * 16
                final[pl.ds(pair * 16, 16)] = rmain[slot, 0, pl.ds(source, 16)].astype(F32)
        else:
            final[...] = rmain[slot, 0].astype(F32)
        for number, there in enumerate((has_next, has_prev)):

            @pl.when(there)
            def _():
                for half in range(2) if slot < FAR else (1,):
                    arrived(
                        rhalo.at[slot, edge_parts(rows, half)[number]],
                        ghalo_recv.at[slot, number, half],
                    )
                for pair in range(rows // 2):
                    if slot < FAR:
                        source = (pair % 2) * 6 + pair // 2 + 3 * number
                    else:
                        source = 6 + pair - (0 if number else rows // 2)
                    target = pair if number else ROWS // 2 - rows // 2 + pair
                    final[pl.ds(target * 16, 16)] += rhalo[
                        slot, pl.ds(source * 16, 16)
                    ].astype(F32)

        result[slot, 0] = final[...].astype(BF16)
        result[slot, 1] = rmain[slot, 1]
        pltpu.make_async_copy(result.at[slot], output.at[slot], store.at[slot]).start()

    for slot in range(HEADS):
        for half in range(2) if slot < FAR else (0,):
            upward, downward = halo_copies(slot, half)
            pl.when(has_next)(upward.wait_send)
            pl.when(has_prev)(downward.wait_send)

    def main_sent(slot):
        where, at_home, local = main_copies(slot)
        pl.when(where != me)(lambda: at_home.wait_send())

    for_each(HEADS, main_sent)

    def gmain_sent(i):
        pl.when(i != me)(lambda: gmain_copies(i)[0].wait_send())

    for_each(RING, gmain_sent)

    def edges_sent(rows):
        def one(i):
            for half in range(2) if rows == HALO else (1,):
                pl.when(has_prev)(lambda: ghalo_copies(rows, half, i)[0].wait_send())
                pl.when(has_next)(lambda: ghalo_copies(rows, half, i)[1].wait_send())

        for_each(RING, one)
        for number, there in enumerate((has_down, has_up)):
            pl.when(there)(lambda: near_main()[number].wait_send())
            pl.when(there)(lambda: gnear_main()[number].wait_send())
            for half in range(2) if rows == HALO else (0,):
                pl.when(there)(lambda: near_halo(rows, half)[number].wait_send())
            for half in range(2) if rows == HALO else (1,):
                pl.when(there)(lambda: gnear_halo(rows, half)[number].wait_send())

    by_group(edges_sent)
    for slot in range(HEADS):
        pltpu.make_async_copy(result.at[slot], output.at[slot], store.at[slot]).wait()


def shards(queries, key_vectors, values, cotangent, dilation):
    frames, rows, cols, width = queries.shape
    flat = [a.reshape(CELL, width) for a in (queries, key_vectors, values, cotangent)]
    lanes = 2 * WIDTH
    dma = pltpu.SemaphoreType.DMA
    hbm = pl.BlockSpec(memory_space=pl.ANY)
    result = pl.pallas_call(
        functools.partial(main_kernel, lax.axis_size("tm") // RING, lax.axis_size("space")),
        out_shape=jax.ShapeDtypeStruct((HEADS, 2, CELL, lanes), BF16),
        in_specs=[hbm] * 5,
        out_specs=hbm,
        scratch_shapes=[
            pltpu.SMEM((HEADS,), jnp.int32),
        ]
        + [pltpu.VMEM((CELL, width), BF16)] * 4
        + [
            pltpu.VMEM((HEADS, 2, CELL, lanes), BF16),
            pltpu.VMEM((SPAN, 2, CELL, lanes), BF16),
            pltpu.VMEM((SPAN, 2 * EDGE, lanes), BF16),
            pltpu.VMEM((ROWS + 2 * HALO, SPAN * COLS, lanes), BF16),
            pltpu.VMEM((ROWS, RING * COLS, lanes), BF16),
            pltpu.VMEM((2, RING * COLS, SPAN * COLS), F32),
            pltpu.VMEM((2, 4 * RING * COLS, 8 * SPAN * COLS), F32),
            pltpu.VMEM((2, 4 * RING * COLS, 8 * SPAN * COLS), BF16),
            pltpu.VMEM((ROWS + 2 * HALO, lanes, SPAN * COLS), F32),
            pltpu.VMEM((SPAN, 2, CELL, lanes), BF16),
            pltpu.VMEM((SPAN, 2 * EDGE, lanes), BF16),
            pltpu.VMEM((2, REACH, CELL, lanes), BF16),
            pltpu.VMEM((2, REACH, 2 * EDGE, lanes), BF16),
            pltpu.VMEM((HEADS, 2, CELL, lanes), BF16),
            pltpu.VMEM((HEADS, 2 * EDGE, lanes), BF16),
            pltpu.VMEM((CELL, lanes), F32),
            pltpu.VMEM((HEADS, 2, CELL, lanes), BF16),
            dma((5,)),
            dma((HEADS,)),
            dma((HEADS,)),
            dma((RING,)),
            dma((HEADS, 2, 2)),
            dma((RING, 2, 2)),
            dma((6,)),
            dma((6,)),
            dma((RING,)),
            dma((HEADS,)),
            dma((RING, 2, 2)),
            dma((HEADS, 2, 2)),
            dma((6,)),
            dma((6,)),
        ],
        compiler_params=pltpu.CompilerParams(
            collective_id=0, has_side_effects=True, vmem_limit_bytes=56 * 1024 * 1024
        ),
        name="neighbourhood_attention",
    )(dilation, *flat)
    outs = pl.pallas_call(
        unpack_kernel,
        out_shape=[jax.ShapeDtypeStruct((CELL, width), BF16)] * 4,
        in_specs=[hbm] * 2,
        out_specs=[hbm] * 4,
        scratch_shapes=[
            pltpu.SMEM((HEADS,), jnp.int32),
            pltpu.VMEM((HEADS, 2, CELL, lanes), BF16),
        ]
        + [pltpu.VMEM((CELL, width), BF16)] * 4
        + [dma((HEADS + 1,)), dma((4,))],
        compiler_params=pltpu.CompilerParams(vmem_limit_bytes=56 * 1024 * 1024),
        name="unpack_heads",
    )(dilation, result)
    return tuple(a.reshape(frames, rows, cols, width) for a in outs)


def solution(mesh):
    placed = P("tm", "space", None, None)
    return jax.shard_map(
        shards,
        mesh=mesh,
        in_specs=(placed, placed, placed, placed, P()),
        out_specs=(placed, placed, placed, placed),
        check_vma=False,
    )
```

```python
import functools

import jax
import jax.numpy as jnp
from jax import lax
from jax.experimental import pallas as pl
from jax.experimental.pallas import tpu as pltpu
from jax.sharding import PartitionSpec as P

HEADS = 8
WIDTH = 64
ROWS = 16
COLS = 8
RING = 8
REACH = 3
SPAN = 16
CELL = ROWS * COLS
HALO = 12
EDGE = HALO * COLS
MESH = pl.DeviceIdType.MESH
F32 = jnp.float32
BF16 = jnp.bfloat16

HALO_ROWS = (12, 12, 12, 12, 4, 4, 6, 6)
GROUP_ROWS = (12, 4, 6)
FAR = 4
LANES = 4


def own_place(pair, far):
    return jnp.where(far, lax.rem(pair, 2) * 4 + lax.div(pair, 2), pair)


def edge_place(pair, far):
    return jnp.where(far, lax.rem(pair, 2) * 6 + lax.div(pair, 2), pair)


def edge_parts(rows, half):
    if rows == HALO:
        return pl.ds(half * EDGE, EDGE // 2), pl.ds(half * EDGE + EDGE // 2, EDGE // 2), pl.ds(half * EDGE, EDGE)
    size = rows * COLS
    return pl.ds(EDGE - size, size), pl.ds(EDGE, size), pl.ds(EDGE - size, 2 * size)


def own_parts(rows, half):
    if rows == HALO:
        return pl.ds(half * CELL // 2 + 16, EDGE // 2), pl.ds(half * CELL // 2, EDGE // 2)
    size = rows * COLS
    return pl.ds(CELL - size, size), pl.ds(0, size)


def slot_device(slot):
    return 2 * lax.rem(slot, 4) + lax.div(slot, 4)


def head_ranks(dilation):
    steps = [dilation[h] for h in range(HEADS)]
    ranks = []
    for h in range(HEADS):
        rank = jnp.int32(0)
        for other in range(HEADS):
            before = steps[other] <= steps[h] if other < h else steps[other] < steps[h]
            if other != h:
                rank = rank + jnp.where(before, 1, 0)
        ranks.append(rank)
    return ranks


def low_lanes(rows):
    return lax.broadcasted_iota(jnp.int32, (rows, 2 * WIDTH), 1) < WIDTH


def pick(ref, chosen):
    width = 2 * WIDTH
    block = ref[:, pl.ds(0, width)]
    for number in range(1, HEADS // 2):
        here = chosen[2 * number] | chosen[2 * number + 1]
        block = jnp.where(here, ref[:, pl.ds(number * width, width)], block)
    return block.astype(F32)


def pack(dilation, first, second, packed, place):
    ranks = head_ranks(dilation)
    low = low_lanes(CELL)
    for slot in range(HEADS):
        chosen = [ranks[h] == (slot + 4) % HEADS for h in range(HEADS)]
        odd = chosen[1] | chosen[3] | chosen[5] | chosen[7]
        a = pick(first, chosen)
        b = pick(second, chosen)
        a = jnp.where(odd, pltpu.roll(a, WIDTH, 1), a)
        b = jnp.where(odd, b, pltpu.roll(b, WIDTH, 1))
        block = jnp.where(low, a, b).astype(BF16)
        if place == 0 and slot < FAR:
            for pair in range(ROWS // 2):
                target = ((pair % 2) * 4 + pair // 2) * 16
                packed[slot, place, pl.ds(target, 16)] = block[pair * 16 : pair * 16 + 16]
        else:
            packed[slot, place] = block


def unpack_kernel(
    dilation_in,
    result_in,
    attended_out,
    grad_query_out,
    grad_key_out,
    grad_value_out,
    dilation,
    result,
    attended,
    grad_query,
    grad_key,
    grad_value,
    load,
    store,
):
    loads = [
        pltpu.make_async_copy(result_in.at[slot], result.at[slot], load.at[slot])
        for slot in range(HEADS)
    ]
    loads.append(pltpu.make_async_copy(dilation_in, dilation, load.at[HEADS]))
    for copy in loads:
        copy.start()
    for copy in loads:
        copy.wait()
    ranks = head_ranks(dilation)
    low = low_lanes(CELL)
    pairs = ((grad_key, grad_value), (grad_query, attended))
    outs = ((grad_key_out, grad_value_out), (grad_query_out, attended_out))
    stores = []
    for place in range(2):
        first, second = pairs[place]
        for block in range(HEADS // 2):
            slots = [lax.rem(ranks[2 * block + i] + 4, HEADS) for i in range(2)]
            lanes = pl.ds(block * 2 * WIDTH, 2 * WIDTH)
            a = result[slots[0], place].astype(F32)
            b = result[slots[1], place].astype(F32)
            first[:, lanes] = jnp.where(low, a, pltpu.roll(b, WIDTH, 1)).astype(BF16)
            second[:, lanes] = jnp.where(low, pltpu.roll(a, WIDTH, 1), b).astype(BF16)
        for i in range(2):
            copy = pltpu.make_async_copy(pairs[place][i], outs[place][i], store.at[2 * place + i])
            copy.start()
            stores.append(copy)
    for copy in stores:
        copy.wait()


def for_each(count, body, unroll=1):
    def step(i, carry):
        for k in range(unroll):
            body(i * unroll + k)
        return carry

    lax.fori_loop(0, count // unroll, step, 0)


def main_kernel(
    rings,
    blocks,
    dilation_in,
    query_in,
    key_in,
    value_in,
    grad_in,
    output,
    dilation,
    query,
    key,
    value,
    grad,
    packed,
    main,
    hstage,
    keys,
    quers,
    bias,
    scores,
    probs,
    total,
    gmain,
    ghalo,
    cmain,
    chalo,
    rmain,
    rhalo,
    final,
    result,
    load,
    store,
    main_send,
    main_recv,
    halo_send,
    halo_recv,
    near_send,
    near_recv,
    gmain_send,
    gmain_recv,
    ghalo_send,
    ghalo_recv,
    gnear_send,
    gnear_recv,
):
    tm = lax.axis_index("tm")
    space = lax.axis_index("space")
    ring = lax.div(tm, RING)
    me = lax.rem(tm, RING)
    my_slot = lax.rem(me, 2) * 4 + lax.div(me, 2)
    group = jnp.where(lax.rem(me, 2) == 0, 0, jnp.where(me < 4, 1, 2))
    far = group == 0
    step = jnp.where(far, 4, group)
    has_down = ring > 0
    has_up = ring < rings - 1
    has_prev = space > 0
    has_next = space < blocks - 1

    def by_group(body):
        for number, rows in enumerate(GROUP_ROWS):
            pl.when(group == number)(functools.partial(body, rows))

    def send(source, target, send_sem, recv_sem, where):
        return pltpu.make_async_remote_copy(
            src_ref=source,
            dst_ref=target,
            send_sem=send_sem,
            recv_sem=recv_sem,
            device_id=where,
            device_id_type=MESH,
        )

    def arrived(ref, sem):
        pltpu.make_async_copy(ref, ref, sem).wait()

    loads = [
        pltpu.make_async_copy(source, target, load.at[number])
        for number, (source, target) in enumerate(
            (
                (dilation_in, dilation),
                (key_in, key),
                (value_in, value),
                (query_in, query),
                (grad_in, grad),
            )
        )
    ]
    for copy in loads:
        copy.start()

    barrier = pltpu.get_barrier_semaphore()

    def hello(where):
        pl.semaphore_signal(barrier, inc=1, device_id=where, device_id_type=MESH)

    @pl.when(has_next)
    def _():
        for i in range(RING):
            hello({"tm": ring * RING + i, "space": space + 1})

    @pl.when(has_prev)
    def _():
        for i in range(RING):
            hello({"tm": ring * RING + i, "space": space - 1})

    for i in range(1, RING):
        hello({"tm": ring * RING + lax.rem(me + i, RING)})
    pl.when(has_down)(lambda: hello({"tm": tm - RING}))
    pl.when(has_up)(lambda: hello({"tm": tm + RING}))
    for copy in loads[:3]:
        copy.wait()
    pack(dilation, key, value, packed, 0)
    greeted = (
        RING
        - 1
        + jnp.where(has_down, 1, 0)
        + jnp.where(has_up, 1, 0)
        + jnp.where(has_prev, RING, 0)
        + jnp.where(has_next, RING, 0)
    )
    pl.semaphore_wait(barrier, greeted)

    def halo_copies(slot, half):
        top, bottom = own_parts(HALO_ROWS[slot], half)
        lower, upper, _ = edge_parts(HALO_ROWS[slot], half)
        there = ring * RING + 2 * (slot % 4) + slot // 4
        upward = send(
            packed.at[slot, 0, top],
            hstage.at[me + 4, lower],
            halo_send.at[slot, 0, half],
            halo_recv.at[me, 0, half],
            {"tm": there, "space": space + 1},
        )
        downward = send(
            packed.at[slot, 0, bottom],
            hstage.at[me + 4, upper],
            halo_send.at[slot, 1, half],
            halo_recv.at[me, 1, half],
            {"tm": there, "space": space - 1},
        )
        return upward, downward

    def halo_start(slot, half):
        upward, downward = halo_copies(slot, half)
        pl.when(has_next)(upward.start)
        pl.when(has_prev)(downward.start)

    for slot in (4, 5, 6, 7, 0, 1, 2, 3):
        halo_start(slot, 0)

    def main_copies(slot, place):
        where = slot_device(slot)
        source = packed.at[slot, place]
        target = main.at[me + 4, place]
        arrival = main_recv.at[me, place]
        at_home = send(
            source, target, main_send.at[slot, place], arrival, {"tm": ring * RING + where}
        )
        local = pltpu.make_async_copy(source, target, arrival)
        return where, at_home, local

    def main_start(slot, place):
        where, at_home, local = main_copies(slot, place)
        pl.when(where != me)(lambda: at_home.start())
        pl.when(where == me)(lambda: local.start())

    for_each(HEADS, lambda slot: main_start(slot, 0))
    for copy in loads[3:]:
        copy.wait()
    pack(dilation, query, grad, packed, 1)
    for_each(HEADS, lambda slot: main_start(slot, 1))

    def clear(first, count):
        def one(i):
            main[first + i, 0] = jnp.zeros((CELL, 2 * WIDTH), BF16)
            hstage[first + i] = jnp.zeros((2 * EDGE, 2 * WIDTH), BF16)

        for_each(count, one)

    clear(0, 1)
    clear(15, 1)
    pl.when(jnp.logical_not(has_down))(lambda: clear(1, 3))
    pl.when(jnp.logical_not(has_up))(lambda: clear(12, 3))

    def clear_halo(rows):
        halves = range(2) if rows == HALO else range(1)

        def one(i):
            for half in halves:
                for number, missing in enumerate((has_prev, has_next)):
                    part = edge_parts(rows, half)[number]

                    @pl.when(jnp.logical_not(missing))
                    def _():
                        hstage[i + 4, part] = jnp.zeros((part.size, 2 * WIDTH), BF16)

        for_each(RING, one)

    by_group(clear_halo)

    def clear_total(i):
        total[i] = jnp.zeros((2 * WIDTH, 2 * WIDTH), F32)

    for_each(2 * HALO + ROWS, clear_total)

    shape = (RING * COLS, SPAN * COLS)
    query_at = lax.broadcasted_iota(jnp.int32, shape, 0)
    key_at = lax.broadcasted_iota(jnp.int32, shape, 1)
    frame_apart = lax.shift_right_logical(key_at, 3) - lax.shift_right_logical(query_at, 3) - 4
    key_frame = lax.shift_right_logical(key_at, 3) + ring * RING - 4
    col_apart = (key_at & 7) - (query_at & 7)
    seen = (
        (jnp.abs(frame_apart) <= REACH)
        & (key_frame >= 0)
        & (key_frame < rings * RING)
        & (jnp.abs(col_apart) <= REACH * step)
        & ((col_apart & (step - 1)) == 0)
    )
    bias[0] = jnp.where(seen, 0.0, -1e30)
    bias[1] = jnp.full(shape, -1e30, F32)

    def main_wait(i):
        arrived(main.at[i + 4, 0], main_recv.at[i, 0])

    def near_main():
        down = send(
            main.at[pl.ds(4, 3), 0], main.at[pl.ds(12, 3), 0], near_send.at[0], near_recv.at[0],
            {"tm": tm - RING},
        )
        up = send(
            main.at[pl.ds(9, 3), 0], main.at[pl.ds(1, 3), 0], near_send.at[1], near_recv.at[1],
            {"tm": tm + RING},
        )
        return down, up

    def near_halo(rows, half):
        part = edge_parts(rows, half)[2]
        down = send(
            hstage.at[pl.ds(4, 3), part], hstage.at[pl.ds(12, 3), part],
            near_send.at[2 + 2 * half], near_recv.at[2 + 2 * half], {"tm": tm - RING},
        )
        up = send(
            hstage.at[pl.ds(9, 3), part], hstage.at[pl.ds(1, 3), part],
            near_send.at[3 + 2 * half], near_recv.at[3 + 2 * half], {"tm": tm + RING},
        )
        return down, up

    for_each(3, main_wait)
    pl.when(has_down)(lambda: near_main()[0].start())
    for_each(3, lambda i: main_wait(i + 5))
    pl.when(has_up)(lambda: near_main()[1].start())
    for_each(2, lambda i: main_wait(i + 3))
    for slot in range(FAR):
        halo_start(slot, 1)


    def halo_phase(half, rows):
        lower, upper, _ = edge_parts(rows, half)

        def one(i):
            pl.when(has_prev)(lambda: arrived(hstage.at[i + 4, lower], halo_recv.at[i, 0, half]))
            pl.when(has_next)(lambda: arrived(hstage.at[i + 4, upper], halo_recv.at[i, 1, half]))

        for_each(3, one)
        pl.when(has_down)(lambda: near_halo(rows, half)[0].start())
        for_each(3, lambda i: one(i + 5))
        pl.when(has_up)(lambda: near_halo(rows, half)[1].start())
        for_each(2, lambda i: one(i + 3))

    by_group(functools.partial(halo_phase, 0))
    pl.when(has_down)(lambda: near_main()[1].wait_recv())
    pl.when(has_up)(lambda: near_main()[0].wait_recv())

    def two_rows(part, frames):
        wide = part.astype(F32).reshape(frames, 2, COLS, 2 * WIDTH)
        return [wide[:, i].reshape(frames * COLS, 2 * WIDTH).astype(BF16) for i in range(2)]

    def turn_main(pair):
        place = pl.ds(pl.multiple_of(own_place(pair, far) * 16, 16), 16)
        even, odd = two_rows(main[:, 0, place], SPAN)
        keys[HALO + 2 * pair] = even
        keys[HALO + 2 * pair + 1] = odd
        rows = pl.ds(pl.multiple_of(pair * 16, 16), 16)
        even, odd = two_rows(main[pl.ds(4, RING), 1, rows], RING)
        quers[2 * pair] = even
        quers[2 * pair + 1] = odd

    for_each(RING, lambda i: arrived(main.at[i + 4, 1], main_recv.at[i, 1]))
    for_each(ROWS // 2, turn_main, 4)

    def near_halo_wait(half, rows):
        pl.when(has_down)(lambda: near_halo(rows, half)[1].wait_recv())
        pl.when(has_up)(lambda: near_halo(rows, half)[0].wait_recv())

    def turn_halo(pair):
        rows = pl.ds(pl.multiple_of(edge_place(pair, far) * 16, 16), 16)
        even, odd = two_rows(hstage[:, rows], SPAN)
        place = 2 * pair + jnp.where(pair < HALO // 2, 0, ROWS)
        keys[place] = even
        keys[place + 1] = odd

    by_group(functools.partial(near_halo_wait, 0))
    pl.when(far)(lambda: for_each(HALO // 2, lambda i: turn_halo(2 * i), 3))
    pl.when(jnp.logical_not(far))(lambda: for_each(HALO, turn_halo, 3))
    pl.when(far)(lambda: halo_phase(1, HALO))

    low = low_lanes(RING * COLS)
    wide = SPAN * COLS
    tall = RING * COLS
    scale = WIDTH ** -0.5 * 1.4426950408889634
    for part in range(4):
        unseen = pl.ds(0 if part % 2 else 7 * wide, wide)
        for lane in range(LANES):
            probs[lane, pl.ds(part * tall, tall), unseen] = jnp.zeros((tall, wide), BF16)

    def score(lane, first):
        pair = [quers[first], quers[first + step]]
        none = jnp.zeros_like(pair[0])
        left = jnp.concatenate(
            [jnp.where(low, q, none) for q in pair] + [jnp.where(low, none, q) for q in pair], 0
        )
        places = [first + HALO + step * (j - REACH) for j in range(8)]
        block = jnp.concatenate([keys[place] for place in places], 0)
        scores[lane] = lax.dot_general(
            left, block, (((1,), (1,)), ((), ())), preferred_element_type=F32
        )
        return left, places, block

    def soften(lane, places):
        outside = []
        for place in places:
            row = place - HALO + space * ROWS
            outside.append(jnp.where((row < 0) | (row >= blocks * ROWS), 1, 0))
        chunk = 16
        for half in range(2):
            for start in range(0, tall, chunk):
                rows = pl.ds(half * tall + start, chunk)
                grad_rows = pl.ds((2 + half) * tall + start, chunk)
                tiles = range(half, half + 7)
                raw = [
                    scores[lane, rows, pl.ds(j * wide, wide)]
                    + bias[outside[j], pl.ds(start, chunk)]
                    for j in tiles
                ]
                peak = jnp.max(functools.reduce(jnp.maximum, raw), axis=1, keepdims=True)
                power = [jnp.exp2((tile - peak) * scale) for tile in raw]
                gains = [scores[lane, grad_rows, pl.ds(j * wide, wide)] for j in tiles]
                summed = jnp.sum(functools.reduce(jnp.add, power), axis=1, keepdims=True)
                inverse = 1.0 / summed
                delta = inverse * jnp.sum(
                    functools.reduce(jnp.add, [a * b for a, b in zip(power, gains)]),
                    axis=1,
                    keepdims=True,
                )
                for j, a, b in zip(tiles, power, gains):
                    weight = a * inverse
                    probs[lane, grad_rows, pl.ds(j * wide, wide)] = weight.astype(BF16)
                    probs[lane, rows, pl.ds(j * wide, wide)] = (weight * (b - delta)).astype(BF16)

    def gather(lane, first, left, places, block):
        both = probs[lane]
        out = jnp.dot(both, block, preferred_element_type=F32)
        for half in range(2):
            grad_query = out[half * tall : (half + 1) * tall] * WIDTH ** -0.5
            attended = out[(2 + half) * tall : (3 + half) * tall]
            quers[first + half * step] = jnp.where(low, grad_query, attended).astype(BF16)
        back = lax.dot_general(left, both, (((0,), (0,)), ((), ())), preferred_element_type=F32)
        for j, place in enumerate(places):
            total[place] += back[:, j * wide : (j + 1) * wide]

    def attend(turn):
        firsts = []
        for lane in range(LANES):
            near = LANES * turn + lane
            apart = (lane // 2) * 4 + lane % 2 + 2 * turn
            i = jnp.where(far, apart, near)
            firsts.append(lax.div(i, step) * (2 * step) + lax.rem(i, step))
        scored = [score(lane, firsts[lane]) for lane in range(LANES)]
        for lane in range(LANES):
            soften(lane, scored[lane][1])
            gather(lane, firsts[lane], *scored[lane])

    low_all = low_lanes(SPAN * COLS)

    def key_row(place):
        turned = total[place].T
        return jnp.where(low_all, turned * WIDTH ** -0.5, turned).reshape(SPAN, COLS, 2 * WIDTH)

    def back_halo(pair):
        place = 2 * pair + jnp.where(pair < HALO // 2, 0, ROWS)
        both = jnp.concatenate([key_row(place), key_row(place + 1)], 1)
        ghalo[:, pl.ds(pl.multiple_of(edge_place(pair, far) * 16, 16), 16)] = both.astype(BF16)

    def gnear_halo(rows, half):
        part = edge_parts(rows, half)[2]
        down = send(
            ghalo.at[pl.ds(1, 3), part], chalo.at[1, :, part],
            gnear_send.at[2 + 2 * half], gnear_recv.at[2 + 2 * half], {"tm": tm - RING},
        )
        up = send(
            ghalo.at[pl.ds(12, 3), part], chalo.at[0, :, part],
            gnear_send.at[3 + 2 * half], gnear_recv.at[3 + 2 * half], {"tm": tm + RING},
        )
        return down, up

    def gnear_main():
        down = send(
            gmain.at[pl.ds(1, 3), 0], cmain.at[1], gnear_send.at[0], gnear_recv.at[0],
            {"tm": tm - RING},
        )
        up = send(
            gmain.at[pl.ds(12, 3), 0], cmain.at[0], gnear_send.at[1], gnear_recv.at[1],
            {"tm": tm + RING},
        )
        return down, up

    def gnear_start(half, rows):
        pl.when(has_down)(lambda: gnear_halo(rows, half)[0].start())
        pl.when(has_up)(lambda: gnear_halo(rows, half)[1].start())

    def back_main(pair):
        rows = pl.ds(pl.multiple_of(pair * 16, 16), 16)
        place = HALO + 2 * pair
        both = jnp.concatenate([key_row(place), key_row(place + 1)], 1)
        gmain[:, 0, pl.ds(pl.multiple_of(own_place(pair, far) * 16, 16), 16)] = both.astype(BF16)
        outs = [quers[2 * pair + i].astype(F32).reshape(RING, COLS, 2 * WIDTH) for i in range(2)]
        gmain[pl.ds(4, RING), 1, rows] = jnp.concatenate(outs, 1).astype(BF16)

    def ghalo_copies(rows, half, i):
        lower, upper, _ = edge_parts(rows, half)
        there = ring * RING + i
        downward = send(
            ghalo.at[i + 4, lower], rhalo.at[my_slot, lower], ghalo_send.at[i, 0, half],
            ghalo_recv.at[my_slot, 0, half], {"tm": there, "space": space - 1},
        )
        upward = send(
            ghalo.at[i + 4, upper], rhalo.at[my_slot, upper], ghalo_send.at[i, 1, half],
            ghalo_recv.at[my_slot, 1, half], {"tm": there, "space": space + 1},
        )
        return downward, upward

    def ghalo_start(half, rows, i):
        pl.when(has_prev)(lambda: ghalo_copies(rows, half, i)[0].start())
        pl.when(has_next)(lambda: ghalo_copies(rows, half, i)[1].start())

    def add_halo(half, rows):
        part = edge_parts(rows, half)[2]

        def add(first, side):
            def one(i):
                both = ghalo[first + i, part].astype(F32) + chalo[side, i, part].astype(F32)
                ghalo[first + i, part] = both.astype(BF16)

            for_each(3, one)

        for_each(2, lambda i: ghalo_start(half, rows, i + 3))

        @pl.when(has_down)
        def _():
            gnear_halo(rows, half)[1].wait_recv()
            add(4, 0)

        for_each(3, lambda i: ghalo_start(half, rows, i))

        @pl.when(has_up)
        def _():
            gnear_halo(rows, half)[0].wait_recv()
            add(9, 1)

        for_each(3, lambda i: ghalo_start(half, rows, i + 5))

    def advance(turn):
        @pl.when(far & (turn == 1))
        def _():
            near_halo_wait(1, HALO)
            for_each(HALO // 2, lambda i: turn_halo(2 * i + 1), 3)

        attend(turn)

        @pl.when(far & (turn == 0))
        def _():
            for_each(HALO // 2, lambda i: back_halo(2 * i), 3)
            gnear_start(0, HALO)

    for_each(2, advance)

    pl.when(far)(lambda: for_each(HALO // 2, lambda i: back_halo(2 * i + 1), 3))
    pl.when(jnp.logical_not(far))(lambda: for_each(HALO, back_halo, 3))
    by_group(functools.partial(gnear_start, 1))
    pl.when(far)(lambda: add_halo(0, HALO))
    for_each(ROWS // 2, back_main, 4)
    pl.when(has_down)(lambda: gnear_main()[0].start())
    pl.when(has_up)(lambda: gnear_main()[1].start())
    by_group(functools.partial(add_halo, 1))

    def gmain_copies(i):
        at_home = send(
            gmain.at[i + 4], rmain.at[my_slot], gmain_send.at[i], gmain_recv.at[my_slot],
            {"tm": ring * RING + i},
        )
        local = pltpu.make_async_copy(gmain.at[i + 4], rmain.at[my_slot], gmain_recv.at[my_slot])
        return at_home, local

    def gmain_start(i):
        pl.when(i != me)(lambda: gmain_copies(i)[0].start())
        pl.when(i == me)(lambda: gmain_copies(i)[1].start())

    def add_main(first, side):
        def one(i):
            both = gmain[first + i, 0].astype(F32) + cmain[side, i].astype(F32)
            gmain[first + i, 0] = both.astype(BF16)

        for_each(3, one)

    for_each(2, lambda i: gmain_start(i + 3))

    @pl.when(has_down)
    def _():
        gnear_main()[1].wait_recv()
        add_main(4, 0)

    for_each(3, gmain_start)

    @pl.when(has_up)
    def _():
        gnear_main()[0].wait_recv()
        add_main(9, 1)

    for_each(3, lambda i: gmain_start(i + 5))

    for slot in (4, 5, 6, 7, 0, 1, 2, 3):
        rows = HALO_ROWS[slot]
        arrived(rmain.at[slot], gmain_recv.at[slot])
        if slot < FAR:
            for pair in range(ROWS // 2):
                source = ((pair % 2) * 4 + pair // 2) * 16
                final[pl.ds(pair * 16, 16)] = rmain[slot, 0, pl.ds(source, 16)].astype(F32)
        else:
            final[...] = rmain[slot, 0].astype(F32)
        for number, there in enumerate((has_next, has_prev)):

            @pl.when(there)
            def _():
                for half in range(2) if slot < FAR else (1,):
                    arrived(
                        rhalo.at[slot, edge_parts(rows, half)[number]],
                        ghalo_recv.at[slot, number, half],
                    )
                for pair in range(rows // 2):
                    if slot < FAR:
                        source = (pair % 2) * 6 + pair // 2 + 3 * number
                    else:
                        source = 6 + pair - (0 if number else rows // 2)
                    target = pair if number else ROWS // 2 - rows // 2 + pair
                    final[pl.ds(target * 16, 16)] += rhalo[
                        slot, pl.ds(source * 16, 16)
                    ].astype(F32)

        result[slot, 0] = final[...].astype(BF16)
        result[slot, 1] = rmain[slot, 1]
        pltpu.make_async_copy(result.at[slot], output.at[slot], store.at[slot]).start()

    for slot in range(HEADS):
        for half in range(2) if slot < FAR else (0,):
            upward, downward = halo_copies(slot, half)
            pl.when(has_next)(upward.wait_send)
            pl.when(has_prev)(downward.wait_send)

    def main_sent(slot):
        for place in range(2):
            where, at_home, local = main_copies(slot, place)
            pl.when(where != me)(lambda: at_home.wait_send())

    for_each(HEADS, main_sent)

    def gmain_sent(i):
        pl.when(i != me)(lambda: gmain_copies(i)[0].wait_send())

    for_each(RING, gmain_sent)

    def edges_sent(rows):
        def one(i):
            for half in range(2) if rows == HALO else (1,):
                pl.when(has_prev)(lambda: ghalo_copies(rows, half, i)[0].wait_send())
                pl.when(has_next)(lambda: ghalo_copies(rows, half, i)[1].wait_send())

        for_each(RING, one)
        for number, there in enumerate((has_down, has_up)):
            pl.when(there)(lambda: near_main()[number].wait_send())
            pl.when(there)(lambda: gnear_main()[number].wait_send())
            for half in range(2) if rows == HALO else (0,):
                pl.when(there)(lambda: near_halo(rows, half)[number].wait_send())
            for half in range(2) if rows == HALO else (1,):
                pl.when(there)(lambda: gnear_halo(rows, half)[number].wait_send())

    by_group(edges_sent)
    for slot in range(HEADS):
        pltpu.make_async_copy(result.at[slot], output.at[slot], store.at[slot]).wait()


def shards(queries, key_vectors, values, cotangent, dilation):
    frames, rows, cols, width = queries.shape
    flat = [a.reshape(CELL, width) for a in (queries, key_vectors, values, cotangent)]
    lanes = 2 * WIDTH
    dma = pltpu.SemaphoreType.DMA
    hbm = pl.BlockSpec(memory_space=pl.ANY)
    result = pl.pallas_call(
        functools.partial(main_kernel, lax.axis_size("tm") // RING, lax.axis_size("space")),
        out_shape=jax.ShapeDtypeStruct((HEADS, 2, CELL, lanes), BF16),
        in_specs=[hbm] * 5,
        out_specs=hbm,
        scratch_shapes=[
            pltpu.SMEM((HEADS,), jnp.int32),
        ]
        + [pltpu.VMEM((CELL, width), BF16)] * 4
        + [
            pltpu.VMEM((HEADS, 2, CELL, lanes), BF16),
            pltpu.VMEM((SPAN, 2, CELL, lanes), BF16),
            pltpu.VMEM((SPAN, 2 * EDGE, lanes), BF16),
            pltpu.VMEM((ROWS + 2 * HALO, SPAN * COLS, lanes), BF16),
            pltpu.VMEM((ROWS, RING * COLS, lanes), BF16),
            pltpu.VMEM((2, RING * COLS, SPAN * COLS), F32),
            pltpu.VMEM((LANES, 4 * RING * COLS, 8 * SPAN * COLS), F32),
            pltpu.VMEM((LANES, 4 * RING * COLS, 8 * SPAN * COLS), BF16),
            pltpu.VMEM((ROWS + 2 * HALO, lanes, SPAN * COLS), F32),
            pltpu.VMEM((SPAN, 2, CELL, lanes), BF16),
            pltpu.VMEM((SPAN, 2 * EDGE, lanes), BF16),
            pltpu.VMEM((2, REACH, CELL, lanes), BF16),
            pltpu.VMEM((2, REACH, 2 * EDGE, lanes), BF16),
            pltpu.VMEM((HEADS, 2, CELL, lanes), BF16),
            pltpu.VMEM((HEADS, 2 * EDGE, lanes), BF16),
            pltpu.VMEM((CELL, lanes), F32),
            pltpu.VMEM((HEADS, 2, CELL, lanes), BF16),
            dma((5,)),
            dma((HEADS,)),
            dma((HEADS, 2)),
            dma((RING, 2)),
            dma((HEADS, 2, 2)),
            dma((RING, 2, 2)),
            dma((6,)),
            dma((6,)),
            dma((RING,)),
            dma((HEADS,)),
            dma((RING, 2, 2)),
            dma((HEADS, 2, 2)),
            dma((6,)),
            dma((6,)),
        ],
        compiler_params=pltpu.CompilerParams(
            collective_id=0, has_side_effects=True, vmem_limit_bytes=56 * 1024 * 1024
        ),
        name="neighbourhood_attention",
    )(dilation, *flat)
    outs = pl.pallas_call(
        unpack_kernel,
        out_shape=[jax.ShapeDtypeStruct((CELL, width), BF16)] * 4,
        in_specs=[hbm] * 2,
        out_specs=[hbm] * 4,
        scratch_shapes=[
            pltpu.SMEM((HEADS,), jnp.int32),
            pltpu.VMEM((HEADS, 2, CELL, lanes), BF16),
        ]
        + [pltpu.VMEM((CELL, width), BF16)] * 4
        + [dma((HEADS + 1,)), dma((4,))],
        compiler_params=pltpu.CompilerParams(vmem_limit_bytes=56 * 1024 * 1024),
        name="unpack_heads",
    )(dilation, result)
    return tuple(a.reshape(frames, rows, cols, width) for a in outs)


def solution(mesh):
    placed = P("tm", "space", None, None)
    return jax.shard_map(
        shards,
        mesh=mesh,
        in_specs=(placed, placed, placed, placed, P()),
        out_specs=(placed, placed, placed, placed),
        check_vma=False,
    )
```

```python
import functools

import jax
import jax.numpy as jnp
from jax import lax
from jax.experimental import pallas as pl
from jax.experimental.pallas import tpu as pltpu
from jax.sharding import PartitionSpec as P

HEADS = 8
WIDTH = 64
ROWS = 16
COLS = 8
RING = 8
REACH = 3
SPAN = 16
CELL = ROWS * COLS
HALO = 12
EDGE = HALO * COLS
MESH = pl.DeviceIdType.MESH
F32 = jnp.float32
BF16 = jnp.bfloat16

HALO_ROWS = (12, 12, 12, 12, 4, 4, 6, 6)
GROUP_ROWS = (12, 4, 6)
FAR = 4
LANES = 4


def own_place(pair, far):
    return jnp.where(far, lax.rem(pair, 2) * 4 + lax.div(pair, 2), pair)


def edge_place(pair, far):
    return jnp.where(far, lax.rem(pair, 2) * 6 + lax.div(pair, 2), pair)


def edge_parts(rows, half):
    if rows == HALO:
        return pl.ds(half * EDGE, EDGE // 2), pl.ds(half * EDGE + EDGE // 2, EDGE // 2), pl.ds(half * EDGE, EDGE)
    size = rows * COLS
    return pl.ds(EDGE - size, size), pl.ds(EDGE, size), pl.ds(EDGE - size, 2 * size)


def own_parts(rows, half):
    if rows == HALO:
        return pl.ds(half * CELL // 2 + 16, EDGE // 2), pl.ds(half * CELL // 2, EDGE // 2)
    size = rows * COLS
    return pl.ds(CELL - size, size), pl.ds(0, size)


def slot_device(slot):
    return 2 * lax.rem(slot, 4) + lax.div(slot, 4)


def head_ranks(dilation):
    steps = [dilation[h] for h in range(HEADS)]
    ranks = []
    for h in range(HEADS):
        rank = jnp.int32(0)
        for other in range(HEADS):
            before = steps[other] <= steps[h] if other < h else steps[other] < steps[h]
            if other != h:
                rank = rank + jnp.where(before, 1, 0)
        ranks.append(rank)
    return ranks


def low_lanes(rows):
    return lax.broadcasted_iota(jnp.int32, (rows, 2 * WIDTH), 1) < WIDTH


def pick(ref, chosen):
    width = 2 * WIDTH
    block = ref[:, pl.ds(0, width)]
    for number in range(1, HEADS // 2):
        here = chosen[2 * number] | chosen[2 * number + 1]
        block = jnp.where(here, ref[:, pl.ds(number * width, width)], block)
    return block.astype(F32)


def pack(dilation, first, second, packed, place):
    ranks = head_ranks(dilation)
    low = low_lanes(CELL)
    for slot in range(HEADS):
        chosen = [ranks[h] == (slot + 4) % HEADS for h in range(HEADS)]
        odd = chosen[1] | chosen[3] | chosen[5] | chosen[7]
        a = pick(first, chosen)
        b = pick(second, chosen)
        a = jnp.where(odd, pltpu.roll(a, WIDTH, 1), a)
        b = jnp.where(odd, b, pltpu.roll(b, WIDTH, 1))
        block = jnp.where(low, a, b).astype(BF16)
        if place == 0 and slot < FAR:
            for pair in range(ROWS // 2):
                target = ((pair % 2) * 4 + pair // 2) * 16
                packed[slot, place, pl.ds(target, 16)] = block[pair * 16 : pair * 16 + 16]
        else:
            packed[slot, place] = block


def unpack_kernel(
    dilation_in,
    result_in,
    attended_out,
    grad_query_out,
    grad_key_out,
    grad_value_out,
    dilation,
    result,
    attended,
    grad_query,
    grad_key,
    grad_value,
    load,
    store,
):
    order = pltpu.make_async_copy(dilation_in, dilation, load.at[2 * HEADS])
    order.start()
    loads = [
        [
            pltpu.make_async_copy(
                result_in.at[slot, place], result.at[slot, place], load.at[place * HEADS + slot]
            )
            for slot in range(HEADS)
        ]
        for place in range(2)
    ]
    for place in (1, 0):
        for copy in loads[place]:
            copy.start()
    order.wait()
    ranks = head_ranks(dilation)
    low = low_lanes(CELL)
    pairs = ((grad_key, grad_value), (grad_query, attended))
    outs = ((grad_key_out, grad_value_out), (grad_query_out, attended_out))
    stores = []
    for place in (1, 0):
        for copy in loads[place]:
            copy.wait()
        first, second = pairs[place]
        for block in range(HEADS // 2):
            slots = [lax.rem(ranks[2 * block + i] + 4, HEADS) for i in range(2)]
            lanes = pl.ds(block * 2 * WIDTH, 2 * WIDTH)
            a = result[slots[0], place].astype(F32)
            b = result[slots[1], place].astype(F32)
            first[:, lanes] = jnp.where(low, a, pltpu.roll(b, WIDTH, 1)).astype(BF16)
            second[:, lanes] = jnp.where(low, pltpu.roll(a, WIDTH, 1), b).astype(BF16)
        for i in range(2):
            copy = pltpu.make_async_copy(pairs[place][i], outs[place][i], store.at[2 * place + i])
            copy.start()
            stores.append(copy)
    for copy in stores:
        copy.wait()


def for_each(count, body, unroll=1):
    def step(i, carry):
        for k in range(unroll):
            body(i * unroll + k)
        return carry

    lax.fori_loop(0, count // unroll, step, 0)


def main_kernel(
    rings,
    blocks,
    dilation_in,
    query_in,
    key_in,
    value_in,
    grad_in,
    output,
    dilation,
    query,
    key,
    value,
    grad,
    packed,
    main,
    hstage,
    keys,
    quers,
    bias,
    scores,
    probs,
    total,
    gmain,
    ghalo,
    cmain,
    chalo,
    rmain,
    rhalo,
    final,
    result,
    load,
    store,
    main_send,
    main_recv,
    halo_send,
    halo_recv,
    near_send,
    near_recv,
    gmain_send,
    gmain_recv,
    ghalo_send,
    ghalo_recv,
    gnear_send,
    gnear_recv,
):
    tm = lax.axis_index("tm")
    space = lax.axis_index("space")
    ring = lax.div(tm, RING)
    me = lax.rem(tm, RING)
    my_slot = lax.rem(me, 2) * 4 + lax.div(me, 2)
    group = jnp.where(lax.rem(me, 2) == 0, 0, jnp.where(me < 4, 1, 2))
    far = group == 0
    step = jnp.where(far, 4, group)
    has_down = ring > 0
    has_up = ring < rings - 1
    has_prev = space > 0
    has_next = space < blocks - 1

    def by_group(body):
        for number, rows in enumerate(GROUP_ROWS):
            pl.when(group == number)(functools.partial(body, rows))

    def send(source, target, send_sem, recv_sem, where):
        return pltpu.make_async_remote_copy(
            src_ref=source,
            dst_ref=target,
            send_sem=send_sem,
            recv_sem=recv_sem,
            device_id=where,
            device_id_type=MESH,
        )

    def arrived(ref, sem):
        pltpu.make_async_copy(ref, ref, sem).wait()

    loads = [
        pltpu.make_async_copy(source, target, load.at[number])
        for number, (source, target) in enumerate(
            (
                (dilation_in, dilation),
                (key_in, key),
                (value_in, value),
                (query_in, query),
                (grad_in, grad),
            )
        )
    ]
    for copy in loads:
        copy.start()

    barrier = pltpu.get_barrier_semaphore()

    def hello(where):
        pl.semaphore_signal(barrier, inc=1, device_id=where, device_id_type=MESH)

    @pl.when(has_next)
    def _():
        for i in range(RING):
            hello({"tm": ring * RING + i, "space": space + 1})

    @pl.when(has_prev)
    def _():
        for i in range(RING):
            hello({"tm": ring * RING + i, "space": space - 1})

    for i in range(1, RING):
        hello({"tm": ring * RING + lax.rem(me + i, RING)})
    pl.when(has_down)(lambda: hello({"tm": tm - RING}))
    pl.when(has_up)(lambda: hello({"tm": tm + RING}))
    for copy in loads[:3]:
        copy.wait()
    pack(dilation, key, value, packed, 0)
    greeted = (
        RING
        - 1
        + jnp.where(has_down, 1, 0)
        + jnp.where(has_up, 1, 0)
        + jnp.where(has_prev, RING, 0)
        + jnp.where(has_next, RING, 0)
    )
    pl.semaphore_wait(barrier, greeted)

    def halo_copies(slot, half):
        top, bottom = own_parts(HALO_ROWS[slot], half)
        lower, upper, _ = edge_parts(HALO_ROWS[slot], half)
        there = ring * RING + 2 * (slot % 4) + slot // 4
        upward = send(
            packed.at[slot, 0, top],
            hstage.at[me + 4, lower],
            halo_send.at[slot, 0, half],
            halo_recv.at[me, 0, half],
            {"tm": there, "space": space + 1},
        )
        downward = send(
            packed.at[slot, 0, bottom],
            hstage.at[me + 4, upper],
            halo_send.at[slot, 1, half],
            halo_recv.at[me, 1, half],
            {"tm": there, "space": space - 1},
        )
        return upward, downward

    def halo_start(slot, half):
        upward, downward = halo_copies(slot, half)
        pl.when(has_next)(upward.start)
        pl.when(has_prev)(downward.start)

    for slot in (4, 5, 6, 7, 0, 1, 2, 3):
        halo_start(slot, 0)

    def main_copies(slot, place):
        where = slot_device(slot)
        source = packed.at[slot, place]
        target = main.at[me + 4, place]
        arrival = main_recv.at[me, place]
        at_home = send(
            source, target, main_send.at[slot, place], arrival, {"tm": ring * RING + where}
        )
        local = pltpu.make_async_copy(source, target, arrival)
        return where, at_home, local

    def main_start(slot, place):
        where, at_home, local = main_copies(slot, place)
        pl.when(where != me)(lambda: at_home.start())
        pl.when(where == me)(lambda: local.start())

    for_each(HEADS, lambda slot: main_start(slot, 0))
    for copy in loads[3:]:
        copy.wait()
    pack(dilation, query, grad, packed, 1)
    for_each(HEADS, lambda slot: main_start(slot, 1))

    def clear(first, count):
        def one(i):
            main[first + i, 0] = jnp.zeros((CELL, 2 * WIDTH), BF16)
            hstage[first + i] = jnp.zeros((2 * EDGE, 2 * WIDTH), BF16)

        for_each(count, one)

    clear(0, 1)
    clear(15, 1)
    pl.when(jnp.logical_not(has_down))(lambda: clear(1, 3))
    pl.when(jnp.logical_not(has_up))(lambda: clear(12, 3))

    def clear_halo(rows):
        halves = range(2) if rows == HALO else range(1)

        def one(i):
            for half in halves:
                for number, missing in enumerate((has_prev, has_next)):
                    part = edge_parts(rows, half)[number]

                    @pl.when(jnp.logical_not(missing))
                    def _():
                        hstage[i + 4, part] = jnp.zeros((part.size, 2 * WIDTH), BF16)

        for_each(RING, one)

    by_group(clear_halo)

    def clear_total(i):
        total[i] = jnp.zeros((2 * WIDTH, 2 * WIDTH), F32)

    for_each(2 * HALO + ROWS, clear_total)

    shape = (RING * COLS, SPAN * COLS)
    query_at = lax.broadcasted_iota(jnp.int32, shape, 0)
    key_at = lax.broadcasted_iota(jnp.int32, shape, 1)
    frame_apart = lax.shift_right_logical(key_at, 3) - lax.shift_right_logical(query_at, 3) - 4
    key_frame = lax.shift_right_logical(key_at, 3) + ring * RING - 4
    col_apart = (key_at & 7) - (query_at & 7)
    seen = (
        (jnp.abs(frame_apart) <= REACH)
        & (key_frame >= 0)
        & (key_frame < rings * RING)
        & (jnp.abs(col_apart) <= REACH * step)
        & ((col_apart & (step - 1)) == 0)
    )
    bias[0] = jnp.where(seen, 0.0, -1e30)
    bias[1] = jnp.full(shape, -1e30, F32)

    def main_wait(i):
        arrived(main.at[i + 4, 0], main_recv.at[i, 0])

    def near_main():
        down = send(
            main.at[pl.ds(4, 3), 0], main.at[pl.ds(12, 3), 0], near_send.at[0], near_recv.at[0],
            {"tm": tm - RING},
        )
        up = send(
            main.at[pl.ds(9, 3), 0], main.at[pl.ds(1, 3), 0], near_send.at[1], near_recv.at[1],
            {"tm": tm + RING},
        )
        return down, up

    def near_halo(rows, half):
        part = edge_parts(rows, half)[2]
        down = send(
            hstage.at[pl.ds(4, 3), part], hstage.at[pl.ds(12, 3), part],
            near_send.at[2 + 2 * half], near_recv.at[2 + 2 * half], {"tm": tm - RING},
        )
        up = send(
            hstage.at[pl.ds(9, 3), part], hstage.at[pl.ds(1, 3), part],
            near_send.at[3 + 2 * half], near_recv.at[3 + 2 * half], {"tm": tm + RING},
        )
        return down, up

    for_each(3, main_wait)
    pl.when(has_down)(lambda: near_main()[0].start())
    for_each(3, lambda i: main_wait(i + 5))
    pl.when(has_up)(lambda: near_main()[1].start())
    for_each(2, lambda i: main_wait(i + 3))
    for slot in range(FAR):
        halo_start(slot, 1)


    def halo_phase(half, rows):
        lower, upper, _ = edge_parts(rows, half)

        def one(i):
            pl.when(has_prev)(lambda: arrived(hstage.at[i + 4, lower], halo_recv.at[i, 0, half]))
            pl.when(has_next)(lambda: arrived(hstage.at[i + 4, upper], halo_recv.at[i, 1, half]))

        for_each(3, one)
        pl.when(has_down)(lambda: near_halo(rows, half)[0].start())
        for_each(3, lambda i: one(i + 5))
        pl.when(has_up)(lambda: near_halo(rows, half)[1].start())
        for_each(2, lambda i: one(i + 3))

    by_group(functools.partial(halo_phase, 0))
    pl.when(has_down)(lambda: near_main()[1].wait_recv())
    pl.when(has_up)(lambda: near_main()[0].wait_recv())

    def two_rows(part, frames):
        wide = part.astype(F32).reshape(frames, 2, COLS, 2 * WIDTH)
        return [wide[:, i].reshape(frames * COLS, 2 * WIDTH).astype(BF16) for i in range(2)]

    def turn_main(pair):
        place = pl.ds(pl.multiple_of(own_place(pair, far) * 16, 16), 16)
        even, odd = two_rows(main[:, 0, place], SPAN)
        keys[HALO + 2 * pair] = even
        keys[HALO + 2 * pair + 1] = odd
        rows = pl.ds(pl.multiple_of(pair * 16, 16), 16)
        even, odd = two_rows(main[pl.ds(4, RING), 1, rows], RING)
        quers[2 * pair] = even
        quers[2 * pair + 1] = odd

    for_each(RING, lambda i: arrived(main.at[i + 4, 1], main_recv.at[i, 1]))
    for_each(ROWS // 2, turn_main, 4)

    def near_halo_wait(half, rows):
        pl.when(has_down)(lambda: near_halo(rows, half)[1].wait_recv())
        pl.when(has_up)(lambda: near_halo(rows, half)[0].wait_recv())

    def turn_halo(pair):
        rows = pl.ds(pl.multiple_of(edge_place(pair, far) * 16, 16), 16)
        even, odd = two_rows(hstage[:, rows], SPAN)
        place = 2 * pair + jnp.where(pair < HALO // 2, 0, ROWS)
        keys[place] = even
        keys[place + 1] = odd

    by_group(functools.partial(near_halo_wait, 0))
    pl.when(far)(lambda: for_each(HALO // 2, lambda i: turn_halo(2 * i), 3))
    pl.when(jnp.logical_not(far))(lambda: for_each(HALO, turn_halo, 3))
    pl.when(far)(lambda: halo_phase(1, HALO))

    low = low_lanes(RING * COLS)
    wide = SPAN * COLS
    tall = RING * COLS
    scale = WIDTH ** -0.5 * 1.4426950408889634
    for part in range(4):
        unseen = pl.ds(0 if part % 2 else 7 * wide, wide)
        for lane in range(LANES):
            probs[lane, pl.ds(part * tall, tall), unseen] = jnp.zeros((tall, wide), BF16)

    def score(lane, first):
        pair = [quers[first], quers[first + step]]
        none = jnp.zeros_like(pair[0])
        left = jnp.concatenate(
            [jnp.where(low, q, none) for q in pair] + [jnp.where(low, none, q) for q in pair], 0
        )
        places = [first + HALO + step * (j - REACH) for j in range(8)]
        block = jnp.concatenate([keys[place] for place in places], 0)
        scores[lane] = lax.dot_general(
            left, block, (((1,), (1,)), ((), ())), preferred_element_type=F32
        )
        return left, places, block

    def soften(lane, places):
        outside = []
        for place in places:
            row = place - HALO + space * ROWS
            outside.append(jnp.where((row < 0) | (row >= blocks * ROWS), 1, 0))
        chunk = 16
        for half in range(2):
            for start in range(0, tall, chunk):
                rows = pl.ds(half * tall + start, chunk)
                grad_rows = pl.ds((2 + half) * tall + start, chunk)
                tiles = range(half, half + 7)
                raw = [
                    scores[lane, rows, pl.ds(j * wide, wide)]
                    + bias[outside[j], pl.ds(start, chunk)]
                    for j in tiles
                ]
                peak = jnp.max(functools.reduce(jnp.maximum, raw), axis=1, keepdims=True)
                power = [jnp.exp2((tile - peak) * scale) for tile in raw]
                gains = [scores[lane, grad_rows, pl.ds(j * wide, wide)] for j in tiles]
                summed = jnp.sum(functools.reduce(jnp.add, power), axis=1, keepdims=True)
                inverse = 1.0 / summed
                delta = inverse * jnp.sum(
                    functools.reduce(jnp.add, [a * b for a, b in zip(power, gains)]),
                    axis=1,
                    keepdims=True,
                )
                for j, a, b in zip(tiles, power, gains):
                    weight = a * inverse
                    probs[lane, grad_rows, pl.ds(j * wide, wide)] = weight.astype(BF16)
                    probs[lane, rows, pl.ds(j * wide, wide)] = (weight * (b - delta)).astype(BF16)

    def gather(lane, first, left, places, block):
        both = probs[lane]
        out = jnp.dot(both, block, preferred_element_type=F32)
        for half in range(2):
            grad_query = out[half * tall : (half + 1) * tall] * WIDTH ** -0.5
            attended = out[(2 + half) * tall : (3 + half) * tall]
            quers[first + half * step] = jnp.where(low, grad_query, attended).astype(BF16)
        back = lax.dot_general(left, both, (((0,), (0,)), ((), ())), preferred_element_type=F32)
        for j, place in enumerate(places):
            total[place] += back[:, j * wide : (j + 1) * wide]

    def attend(turn):
        firsts = []
        for lane in range(LANES):
            near = LANES * turn + lane
            apart = (lane // 2) * 4 + lane % 2 + 2 * turn
            i = jnp.where(far, apart, near)
            firsts.append(lax.div(i, step) * (2 * step) + lax.rem(i, step))
        scored = [score(lane, firsts[lane]) for lane in range(LANES)]
        for lane in range(LANES):
            soften(lane, scored[lane][1])
            gather(lane, firsts[lane], *scored[lane])

    low_all = low_lanes(SPAN * COLS)

    def key_row(place):
        turned = total[place].T
        return jnp.where(low_all, turned * WIDTH ** -0.5, turned).reshape(SPAN, COLS, 2 * WIDTH)

    def back_halo(pair):
        place = 2 * pair + jnp.where(pair < HALO // 2, 0, ROWS)
        both = jnp.concatenate([key_row(place), key_row(place + 1)], 1)
        ghalo[:, pl.ds(pl.multiple_of(edge_place(pair, far) * 16, 16), 16)] = both.astype(BF16)

    def gnear_halo(rows, half):
        part = edge_parts(rows, half)[2]
        down = send(
            ghalo.at[pl.ds(1, 3), part], chalo.at[1, :, part],
            gnear_send.at[2 + 2 * half], gnear_recv.at[2 + 2 * half], {"tm": tm - RING},
        )
        up = send(
            ghalo.at[pl.ds(12, 3), part], chalo.at[0, :, part],
            gnear_send.at[3 + 2 * half], gnear_recv.at[3 + 2 * half], {"tm": tm + RING},
        )
        return down, up

    def gnear_main():
        down = send(
            gmain.at[pl.ds(1, 3), 0], cmain.at[1], gnear_send.at[0], gnear_recv.at[0],
            {"tm": tm - RING},
        )
        up = send(
            gmain.at[pl.ds(12, 3), 0], cmain.at[0], gnear_send.at[1], gnear_recv.at[1],
            {"tm": tm + RING},
        )
        return down, up

    def gnear_start(half, rows):
        pl.when(has_down)(lambda: gnear_halo(rows, half)[0].start())
        pl.when(has_up)(lambda: gnear_halo(rows, half)[1].start())

    def back_main(pair):
        rows = pl.ds(pl.multiple_of(pair * 16, 16), 16)
        place = HALO + 2 * pair
        both = jnp.concatenate([key_row(place), key_row(place + 1)], 1)
        gmain[:, 0, pl.ds(pl.multiple_of(own_place(pair, far) * 16, 16), 16)] = both.astype(BF16)
        outs = [quers[2 * pair + i].astype(F32).reshape(RING, COLS, 2 * WIDTH) for i in range(2)]
        gmain[pl.ds(4, RING), 1, rows] = jnp.concatenate(outs, 1).astype(BF16)

    def ghalo_copies(rows, half, i):
        lower, upper, _ = edge_parts(rows, half)
        there = ring * RING + i
        downward = send(
            ghalo.at[i + 4, lower], rhalo.at[my_slot, lower], ghalo_send.at[i, 0, half],
            ghalo_recv.at[my_slot, 0, half], {"tm": there, "space": space - 1},
        )
        upward = send(
            ghalo.at[i + 4, upper], rhalo.at[my_slot, upper], ghalo_send.at[i, 1, half],
            ghalo_recv.at[my_slot, 1, half], {"tm": there, "space": space + 1},
        )
        return downward, upward

    def ghalo_start(half, rows, i):
        pl.when(has_prev)(lambda: ghalo_copies(rows, half, i)[0].start())
        pl.when(has_next)(lambda: ghalo_copies(rows, half, i)[1].start())

    def add_halo(half, rows):
        part = edge_parts(rows, half)[2]

        def add(first, side):
            def one(i):
                both = ghalo[first + i, part].astype(F32) + chalo[side, i, part].astype(F32)
                ghalo[first + i, part] = both.astype(BF16)

            for_each(3, one)

        for_each(2, lambda i: ghalo_start(half, rows, i + 3))

        @pl.when(has_down)
        def _():
            gnear_halo(rows, half)[1].wait_recv()
            add(4, 0)

        for_each(3, lambda i: ghalo_start(half, rows, i))

        @pl.when(has_up)
        def _():
            gnear_halo(rows, half)[0].wait_recv()
            add(9, 1)

        for_each(3, lambda i: ghalo_start(half, rows, i + 5))

    def advance(turn):
        @pl.when(far & (turn == 1))
        def _():
            near_halo_wait(1, HALO)
            for_each(HALO // 2, lambda i: turn_halo(2 * i + 1), 3)

        attend(turn)

        @pl.when(far & (turn == 0))
        def _():
            for_each(HALO // 2, lambda i: back_halo(2 * i), 3)
            gnear_start(0, HALO)

    for_each(2, advance)

    pl.when(far)(lambda: for_each(HALO // 2, lambda i: back_halo(2 * i + 1), 3))
    pl.when(jnp.logical_not(far))(lambda: for_each(HALO, back_halo, 3))
    by_group(functools.partial(gnear_start, 1))
    pl.when(far)(lambda: add_halo(0, HALO))
    for_each(ROWS // 2, back_main, 4)
    pl.when(has_down)(lambda: gnear_main()[0].start())
    pl.when(has_up)(lambda: gnear_main()[1].start())
    by_group(functools.partial(add_halo, 1))

    def gmain_copies(i):
        at_home = send(
            gmain.at[i + 4], rmain.at[my_slot], gmain_send.at[i], gmain_recv.at[my_slot],
            {"tm": ring * RING + i},
        )
        local = pltpu.make_async_copy(gmain.at[i + 4], rmain.at[my_slot], gmain_recv.at[my_slot])
        return at_home, local

    def gmain_start(i):
        pl.when(i != me)(lambda: gmain_copies(i)[0].start())
        pl.when(i == me)(lambda: gmain_copies(i)[1].start())

    def add_main(first, side):
        def one(i):
            both = gmain[first + i, 0].astype(F32) + cmain[side, i].astype(F32)
            gmain[first + i, 0] = both.astype(BF16)

        for_each(3, one)

    for_each(2, lambda i: gmain_start(i + 3))

    @pl.when(has_down)
    def _():
        gnear_main()[1].wait_recv()
        add_main(4, 0)

    for_each(3, gmain_start)

    @pl.when(has_up)
    def _():
        gnear_main()[0].wait_recv()
        add_main(9, 1)

    for_each(3, lambda i: gmain_start(i + 5))

    for slot in (4, 5, 6, 7, 0, 1, 2, 3):
        rows = HALO_ROWS[slot]
        arrived(rmain.at[slot], gmain_recv.at[slot])
        pltpu.make_async_copy(rmain.at[slot, 1], output.at[slot, 1], store.at[HEADS + slot]).start()
        if slot < FAR:
            for pair in range(ROWS // 2):
                source = ((pair % 2) * 4 + pair // 2) * 16
                final[pl.ds(pair * 16, 16)] = rmain[slot, 0, pl.ds(source, 16)].astype(F32)
        else:
            final[...] = rmain[slot, 0].astype(F32)
        for number, there in enumerate((has_next, has_prev)):

            @pl.when(there)
            def _():
                for half in range(2) if slot < FAR else (1,):
                    arrived(
                        rhalo.at[slot, edge_parts(rows, half)[number]],
                        ghalo_recv.at[slot, number, half],
                    )
                for pair in range(rows // 2):
                    if slot < FAR:
                        source = (pair % 2) * 6 + pair // 2 + 3 * number
                    else:
                        source = 6 + pair - (0 if number else rows // 2)
                    target = pair if number else ROWS // 2 - rows // 2 + pair
                    final[pl.ds(target * 16, 16)] += rhalo[
                        slot, pl.ds(source * 16, 16)
                    ].astype(F32)

        result[slot, 0] = final[...].astype(BF16)
        pltpu.make_async_copy(result.at[slot, 0], output.at[slot, 0], store.at[slot]).start()

    for slot in range(HEADS):
        for half in range(2) if slot < FAR else (0,):
            upward, downward = halo_copies(slot, half)
            pl.when(has_next)(upward.wait_send)
            pl.when(has_prev)(downward.wait_send)

    def main_sent(slot):
        for place in range(2):
            where, at_home, local = main_copies(slot, place)
            pl.when(where != me)(lambda: at_home.wait_send())

    for_each(HEADS, main_sent)

    def gmain_sent(i):
        pl.when(i != me)(lambda: gmain_copies(i)[0].wait_send())

    for_each(RING, gmain_sent)

    def edges_sent(rows):
        def one(i):
            for half in range(2) if rows == HALO else (1,):
                pl.when(has_prev)(lambda: ghalo_copies(rows, half, i)[0].wait_send())
                pl.when(has_next)(lambda: ghalo_copies(rows, half, i)[1].wait_send())

        for_each(RING, one)
        for number, there in enumerate((has_down, has_up)):
            pl.when(there)(lambda: near_main()[number].wait_send())
            pl.when(there)(lambda: gnear_main()[number].wait_send())
            for half in range(2) if rows == HALO else (0,):
                pl.when(there)(lambda: near_halo(rows, half)[number].wait_send())
            for half in range(2) if rows == HALO else (1,):
                pl.when(there)(lambda: gnear_halo(rows, half)[number].wait_send())

    by_group(edges_sent)
    for slot in range(HEADS):
        pltpu.make_async_copy(result.at[slot, 0], output.at[slot, 0], store.at[slot]).wait()
        pltpu.make_async_copy(rmain.at[slot, 1], output.at[slot, 1], store.at[HEADS + slot]).wait()


def shards(queries, key_vectors, values, cotangent, dilation):
    frames, rows, cols, width = queries.shape
    flat = [a.reshape(CELL, width) for a in (queries, key_vectors, values, cotangent)]
    lanes = 2 * WIDTH
    dma = pltpu.SemaphoreType.DMA
    hbm = pl.BlockSpec(memory_space=pl.ANY)
    result = pl.pallas_call(
        functools.partial(main_kernel, lax.axis_size("tm") // RING, lax.axis_size("space")),
        out_shape=jax.ShapeDtypeStruct((HEADS, 2, CELL, lanes), BF16),
        in_specs=[hbm] * 5,
        out_specs=hbm,
        scratch_shapes=[
            pltpu.SMEM((HEADS,), jnp.int32),
        ]
        + [pltpu.VMEM((CELL, width), BF16)] * 4
        + [
            pltpu.VMEM((HEADS, 2, CELL, lanes), BF16),
            pltpu.VMEM((SPAN, 2, CELL, lanes), BF16),
            pltpu.VMEM((SPAN, 2 * EDGE, lanes), BF16),
            pltpu.VMEM((ROWS + 2 * HALO, SPAN * COLS, lanes), BF16),
            pltpu.VMEM((ROWS, RING * COLS, lanes), BF16),
            pltpu.VMEM((2, RING * COLS, SPAN * COLS), F32),
            pltpu.VMEM((LANES, 4 * RING * COLS, 8 * SPAN * COLS), F32),
            pltpu.VMEM((LANES, 4 * RING * COLS, 8 * SPAN * COLS), BF16),
            pltpu.VMEM((ROWS + 2 * HALO, lanes, SPAN * COLS), F32),
            pltpu.VMEM((SPAN, 2, CELL, lanes), BF16),
            pltpu.VMEM((SPAN, 2 * EDGE, lanes), BF16),
            pltpu.VMEM((2, REACH, CELL, lanes), BF16),
            pltpu.VMEM((2, REACH, 2 * EDGE, lanes), BF16),
            pltpu.VMEM((HEADS, 2, CELL, lanes), BF16),
            pltpu.VMEM((HEADS, 2 * EDGE, lanes), BF16),
            pltpu.VMEM((CELL, lanes), F32),
            pltpu.VMEM((HEADS, 2, CELL, lanes), BF16),
            dma((5,)),
            dma((2 * HEADS,)),
            dma((HEADS, 2)),
            dma((RING, 2)),
            dma((HEADS, 2, 2)),
            dma((RING, 2, 2)),
            dma((6,)),
            dma((6,)),
            dma((RING,)),
            dma((HEADS,)),
            dma((RING, 2, 2)),
            dma((HEADS, 2, 2)),
            dma((6,)),
            dma((6,)),
        ],
        compiler_params=pltpu.CompilerParams(
            collective_id=0, has_side_effects=True, vmem_limit_bytes=56 * 1024 * 1024
        ),
        name="neighbourhood_attention",
    )(dilation, *flat)
    outs = pl.pallas_call(
        unpack_kernel,
        out_shape=[jax.ShapeDtypeStruct((CELL, width), BF16)] * 4,
        in_specs=[hbm] * 2,
        out_specs=[hbm] * 4,
        scratch_shapes=[
            pltpu.SMEM((HEADS,), jnp.int32),
            pltpu.VMEM((HEADS, 2, CELL, lanes), BF16),
        ]
        + [pltpu.VMEM((CELL, width), BF16)] * 4
        + [dma((2 * HEADS + 1,)), dma((4,))],
        compiler_params=pltpu.CompilerParams(vmem_limit_bytes=56 * 1024 * 1024),
        name="unpack_heads",
    )(dilation, result)
    return tuple(a.reshape(frames, rows, cols, width) for a in outs)


def solution(mesh):
    placed = P("tm", "space", None, None)
    return jax.shard_map(
        shards,
        mesh=mesh,
        in_specs=(placed, placed, placed, placed, P()),
        out_specs=(placed, placed, placed, placed),
        check_vma=False,
    )
```
